256 devices in a mesh: row: 8 (over z), col: 8 (over x, core), rep: 4 (over y).
Axes of the slice: x: 4, y: 4, z: 8, core: 2. Of those that a mesh axis runs over, the one named last changes fastest.
Arguments:
- features: bfloat16 [65536, 256], P(('col', 'rep'), 'row'), may hold values from -6 to 6
- weight: bfloat16 [256, 256], replicated, may hold values from -0.375 to 0.375
- cotangent: bfloat16 [65536, 256], P(('row', 'col', 'rep')), may hold values from -6 to 6
- block_values: bfloat16 [8, 32, 320, 128, 128], P('row', ('col', 'rep')), may hold values from -0.0390625 to 0.0390625
- block_coords: int32 [8, 32, 320, 2], P('row', ('col', 'rep')), may hold values from 0 to 63, as said below
- block_counts: int32 [8, 32], P('row', ('col', 'rep')), may hold values from 1 to 320, as said below
Outputs:
- activations: bfloat16 [65536, 256], P(('row', 'col', 'rep'))
- input_grad: bfloat16 [65536, 256], P(('col', 'rep'), 'row')
- weight_grad: float32 [256, 256], replicated
The draws below stay inside these ranges and needn't reach their ends.
Inputs may be any that keep to these rules, and one draw needn't show every extreme that they name: `block_coords`: each slot's row block is below 64 and its column block below 16. `block_counts`: some tile uses all 320 slots.
All inputs are finite; a program needn't handle non-finite values.
Results may differ from the reference program's by a relative error of at most 0.014.
Values may be sent and summed in bfloat16 or wider, within the bound.
No kernel may reach another device: no remote copies, remote signals or barrier semaphores. Data moves between devices by JAX's collectives and lax.ppermute only.
A program may use at most 128 MiB of HBM per device.

```python
import jax
import jax.numpy as jnp
from jax import lax

F = 256
NODE_DEV = 256
NODES = 65536
ROW_TILES = 8
COL_TILES = 32
TILE_RB = 64
TILE_CB = 16
NNZB = 320


def draw_block_coords(key, part):
    key_rows = jax.random.fold_in(key, 11)
    key_cols = jax.random.fold_in(key, 12)
    rows_at = jax.random.randint(key_rows, (ROW_TILES, COL_TILES, NNZB), 0, TILE_RB, dtype=jnp.int32)
    cols_at = jax.random.randint(key_cols, (ROW_TILES, COL_TILES, NNZB), 0, TILE_CB, dtype=jnp.int32)
    rows_at = rows_at.at[0, 0, 0].set(TILE_RB - 1)
    cols_at = cols_at.at[0, 0, 0].set(TILE_CB - 1)
    return jnp.stack([rows_at, cols_at], axis=-1)


def draw_block_counts(key, part):
    key_counts = jax.random.fold_in(key, 21)
    key_full = jax.random.fold_in(key, 22)
    lowest = max(1, NNZB // 8)
    counts = jax.random.randint(key_counts, (ROW_TILES * COL_TILES,), lowest, NNZB + 1, dtype=jnp.int32)
    full_at = jax.random.randint(key_full, (), 0, ROW_TILES * COL_TILES, dtype=jnp.int32)
    counts = counts.at[full_at].set(NNZB)
    return counts.reshape(ROW_TILES, COL_TILES)


def levels(rng, extent, split, smallest, high):
    loudness, own = 1.0, jax.random.fold_in(rng, 6)
    for dim, shards_of in split:
        draws = jnp.exp(jax.random.uniform(jax.random.fold_in(own, dim), (shards_of,), jnp.float32, smallest / len(split), high / len(split)))
        loudness = loudness * jnp.repeat(draws, extent[dim] // shards_of).reshape([-1 if axis == dim else 1 for axis in range(len(extent))])
    return loudness


def bell_draw(key, shape, width, bound, cuts=(), kind=jnp.bfloat16):
    level = levels(key, shape, cuts, -0.22, 0.18) if cuts else 1.0
    drawn = jax.random.normal(key, shape, jnp.float32) * width * level
    return jnp.minimum(jnp.maximum(drawn, -bound), bound).astype(kind)


def setup_inputs(seed: int = 0) -> dict:
    seeds = jax.random.split(jax.random.key(seed), 7)
    features = bell_draw(seeds[0], (NODES, F), 1.0, 6.0, ((0, 32), (1, 8)))
    weight = bell_draw(seeds[1], (F, F), F ** -0.5, 0.375)
    cotangent = bell_draw(seeds[2], (NODES, F), 1.0, 6.0, ((0, 256),))
    block_values = bell_draw(seeds[3], (ROW_TILES, COL_TILES, NNZB, 128, 128), (16384 * NNZB // NODE_DEV) ** -0.5, 0.0390625, ((0, 8), (1, 32)))
    block_coords = draw_block_coords(jax.random.fold_in(seeds[6], 71), 0)
    block_counts = draw_block_counts(jax.random.fold_in(seeds[6], 71), 0)
    return {"features": features, "weight": weight, "cotangent": cotangent, "block_values": block_values, "block_coords": block_coords, "block_counts": block_counts}


def reference(features, weight, cotangent, block_values, block_coords, block_counts):
    tiles_total = ROW_TILES * COL_TILES
    blocks = block_values.reshape(tiles_total, NNZB, 128, 128)
    coords = block_coords.reshape(tiles_total, NNZB, 2)
    counts = block_counts.reshape(tiles_total)
    tile_ids = jnp.arange(tiles_total, dtype=jnp.int32)
    slot_ids = jnp.arange(NNZB, dtype=jnp.int32)
    feat_blocks = features.reshape(NODES // 128, 128, F)

    def places(coords_t, tile):
        tile_row = tile // COL_TILES
        tile_col = tile % COL_TILES
        rows_at = (tile_row * TILE_RB + coords_t[:, 0]).astype(jnp.int32)
        cols_at = (tile_col * TILE_CB + coords_t[:, 1]).astype(jnp.int32)
        return rows_at, cols_at

    def forward_step(total, inputs):
        blocks_t, coords_t, count_t, tile = inputs
        rows_at, cols_at = places(coords_t, tile)
        chosen = feat_blocks[cols_at].astype(jnp.float32)
        product = jnp.einsum("bij,bjf->bif", blocks_t.astype(jnp.float32), chosen,
                             precision=lax.Precision.HIGHEST)
        is_live = (slot_ids < count_t).astype(jnp.float32)
        return total.at[rows_at].add(product * is_live[:, None, None]), None

    start = jnp.zeros((NODES // 128, 128, F), jnp.float32)
    total, _ = lax.scan(forward_step, start, (blocks, coords, counts, tile_ids))
    aggregate = total.reshape(NODES, F).astype(jnp.bfloat16)
    pre_act = jnp.dot(aggregate, weight, preferred_element_type=jnp.float32)
    sigma = jax.nn.sigmoid(pre_act)
    activations = (pre_act * sigma).astype(jnp.bfloat16)
    grad_pre = (cotangent.astype(jnp.float32) * sigma * (1.0 + pre_act * (1.0 - sigma))).astype(jnp.bfloat16)
    weight_grad = jnp.dot(aggregate.T, grad_pre, preferred_element_type=jnp.float32)
    back_rows = jnp.dot(grad_pre, weight.T, preferred_element_type=jnp.float32).astype(jnp.bfloat16)
    back_blocks = back_rows.reshape(NODES // 128, 128, F)

    def backward_step(total, inputs):
        blocks_t, coords_t, count_t, tile = inputs
        rows_at, cols_at = places(coords_t, tile)
        chosen = back_blocks[rows_at].astype(jnp.float32)
        product = jnp.einsum("bji,bjf->bif", blocks_t.astype(jnp.float32), chosen,
                             precision=lax.Precision.HIGHEST)
        is_live = (slot_ids < count_t).astype(jnp.float32)
        return total.at[cols_at].add(product * is_live[:, None, None]), None

    total_back, _ = lax.scan(backward_step, start, (blocks, coords, counts, tile_ids))
    input_grad = total_back.reshape(NODES, F).astype(jnp.bfloat16)
    return (activations, input_grad, weight_grad)
```

```python
import functools

import jax
import jax.numpy as jnp
from jax import lax
from jax.experimental import pallas as pl
from jax.experimental.pallas import tpu as pltpu
from jax.sharding import PartitionSpec as P

F32 = jnp.float32
BF16 = jnp.bfloat16
CORES = 2
UNROLL = 4
VMEM = pl.BlockSpec(memory_space=pltpu.VMEM)
SMEM = pl.BlockSpec(memory_space=pltpu.SMEM)


def call(kernel, args, out_shape, scratch=(), smem=0, limit=8 << 20, flops=0):
    moved = sum(a.size * a.dtype.itemsize for a in (*args, *out_shape))
    return pl.pallas_call(
        kernel,
        out_shape=out_shape,
        in_specs=[SMEM] * smem + [VMEM] * (len(args) - smem),
        out_specs=[VMEM] * len(out_shape),
        scratch_shapes=list(scratch),
        compiler_params=pltpu.CompilerParams(vmem_limit_bytes=limit),
        cost_estimate=pl.CostEstimate(flops=flops, bytes_accessed=moved, transcendentals=0),
    )(*args)


def shape(dims, dtype=BF16):
    return jax.ShapeDtypeStruct(dims, dtype)


def added(*arrays):
    total = arrays[0].astype(F32)
    for a in arrays[1:]:
        total = total + a.astype(F32)
    return total.astype(BF16)


def forward_kernel(nz, nx, ny, pos_ref, col_ref, count_ref, at_ref, *refs):
    pieces, (blocks, send_a, send_b, keep_a, keep_b, turned, feat, acc) = refs[:nz], refs[nz:]
    size = blocks.shape[1]
    shard = pieces[0].shape[0]
    half = acc.shape[2] // 2
    z = at_ref[0]
    for dz in range(nz):
        at = pl.multiple_of(lax.rem(z + dz, nz) * shard, shard)
        turned[pl.ds(at, shard), :] = pieces[dz][...]
    for c in range(feat.shape[0]):
        feat[c] = turned[:, c * size : (c + 1) * size].T
    rows = acc.shape[0] - 1

    def clear(r, carry):
        acc[r] = jnp.zeros(acc.shape[1:], F32)
        return carry

    lax.fori_loop(0, rows, clear, 0)
    count = count_ref[0]

    def turn(k, carry):
        products = []
        for u in range(UNROLL):
            s = k * UNROLL + u
            products.append(jnp.dot(blocks[s], feat[col_ref[s]], preferred_element_type=F32))
        for u in range(UNROLL):
            s = k * UNROLL + u
            r = jnp.where(s < count, pos_ref[s], rows)
            acc[r] += products[u]
        return carry

    lax.fori_loop(0, blocks.shape[0] // UNROLL, turn, 0)
    plane = nx * ny
    for c, (out_a, out_b) in enumerate(((keep_a, keep_b), (send_a, send_b))):
        for dx in range(nx):
            for dy in range(ny):
                for part, major, minor in ((0, dx, dy), (1, dy, dx)):
                    for b in range(2):
                        r = (c * plane + dx * ny + dy) * 2 + b
                        value = acc[r, :, part * half : (part + 1) * half].astype(BF16)
                        to = pl.ds(b * size, size)
                        if major == 2:
                            out_a[part, minor, to, :] = value
                        else:
                            out_b[part, (1, 3, 0).index(major), minor, to, :] = value


def first_sum_kernel(keep_a, recv_a, ua, ub, va, vb):
    for part, (low, high) in enumerate(((ua, ub), (va, vb))):
        low[...] = added(keep_a[part, :2], recv_a[part, :2])
        high[...] = added(keep_a[part, 2:], recv_a[part, 2:])


def second_sum_kernel(keep_b, recv_b, ua, ub, va, vb, u1, u3, v1, v3):
    for part, (low, high, o1, o3) in enumerate(((ua, ub, u1, u3), (va, vb, v1, v3))):
        o1[:2] = added(keep_b[part, 0, :2], recv_b[part, 0, :2], low[...])
        o1[2:] = added(keep_b[part, 0, 2:], recv_b[part, 0, 2:])
        o3[:2] = added(keep_b[part, 1, :2], recv_b[part, 1, :2])
        o3[2:] = added(keep_b[part, 1, 2:], recv_b[part, 1, 2:], high[...])


def third_sum_kernel(keep_b, recv_b, um, up, vm, vp, *outs):
    for part, (minus, plus) in enumerate(((um, up), (vm, vp))):
        for d in range(4):
            outs[part * 4 + d][...] = added(
                keep_b[part, 2, d], recv_b[part, 2, d], minus[d], plus[d]
            )


def middle_kernel(nx, ny, at_ref, *refs):
    u, v = refs[:4], refs[4:8]
    weight, cotangent, act, back_u, back_v, w_keep, w_send, agg, terms = refs[8:]
    half = u[0].shape[1]
    for part, arrays in enumerate((u, v)):
        agg[:, part * half : (part + 1) * half] = added(*(a[...] for a in arrays))
    pre = jnp.dot(agg[...], weight[...], preferred_element_type=F32)
    sigma = jax.nn.sigmoid(pre)
    act[...] = (pre * sigma).astype(BF16)
    grad = (cotangent[...].astype(F32) * sigma * (1.0 + pre * (1.0 - sigma))).astype(BF16)
    back = lax.dot_general(
        grad, weight[...], (((1,), (1,)), ((), ())), preferred_element_type=F32
    ).astype(BF16)
    back_u[...] = back[:, :half]
    back_v[...] = back[:, half:]
    terms[...] = lax.dot_general(
        agg[...], grad, (((0,), (0,)), ((), ())), preferred_element_type=F32
    )
    x, core, y = at_ref[1], at_ref[2], at_ref[3]
    step = terms.shape[0] // (CORES * nx * ny)
    for c, out in enumerate((w_keep, w_send)):
        for dx in range(nx):
            for dy in range(ny):
                owner = (jnp.bitwise_xor(core, c) * nx + lax.rem(x + dx, nx)) * ny + lax.rem(y + dy, ny)
                at = pl.multiple_of(owner * step, step)
                out[pl.ds((dx * ny + dy) * step, step), :] = terms[pl.ds(at, step), :]


def place_kernel(nx, ny, at_ref, mine, other, out):
    x, core, y = at_ref[1], at_ref[2], at_ref[3]
    step = out.shape[0] // (CORES * nx * ny)
    for c, piece in enumerate((mine, other)):
        for dx in range(nx):
            for dy in range(ny):
                owner = (jnp.bitwise_xor(core, c) * nx + lax.rem(x + dx, nx)) * ny + lax.rem(y + dy, ny)
                at = pl.multiple_of(owner * step, step)
                out[pl.ds(at, step), :] = piece[pl.ds((dx * ny + dy) * step, step), :]


def stack_kernel(*refs):
    ins, outs = refs[:8], refs[8:]
    for part in range(2):
        for d in range(4):
            outs[part][d] = ins[part * 4 + d][...]


def halves_kernel(xm, xp, ym, yp, *outs):
    for part, (minus, plus) in enumerate(((xm, xp), (ym, yp))):
        outs[part * 2][...] = minus[:2]
        outs[part * 2 + 1][...] = plus[2:]


def backward_kernel(nz, nx, ny, pos_ref, col_ref, count_ref, at_ref, *refs):
    pieces, blocks, outs, (back, acc, turned) = refs[:20], refs[20], refs[21 : 21 + nz], refs[21 + nz :]
    size = blocks.shape[1]
    half = back.shape[2] // 2
    plane = nx * ny
    for c in range(CORES):
        for part in range(2):
            own, minus, plus, low, high = pieces[c * 10 + part * 5 : c * 10 + part * 5 + 5]
            for major in range(4):
                for minor in range(4):
                    source = {0: own, 3: minus, 1: plus, 2: low if minor < 2 else high}[major]
                    k = minor % 2 if major == 2 else minor
                    dx, dy = (major, minor) if part == 0 else (minor, major)
                    for b in range(2):
                        r = (c * plane + dx * ny + dy) * 2 + b
                        back[r, :, part * half : (part + 1) * half] = source[k, b * size : (b + 1) * size, :]
    cols = acc.shape[0] - 1
    for c in range(cols):
        acc[c] = jnp.zeros(acc.shape[1:], F32)
    count = count_ref[0]

    def turn(k, carry):
        products = []
        for u in range(UNROLL):
            s = k * UNROLL + u
            products.append(
                lax.dot_general(
                    blocks[s], back[pos_ref[s]], (((0,), (0,)), ((), ())), preferred_element_type=F32
                )
            )
        for u in range(UNROLL):
            s = k * UNROLL + u
            c = jnp.where(s < count, col_ref[s], cols)
            acc[c] += products[u]
        return carry

    lax.fori_loop(0, blocks.shape[0] // UNROLL, turn, 0)
    for c in range(cols):
        turned[:, c * size : (c + 1) * size] = acc[c].astype(BF16).T
    shard = outs[0].shape[0]
    z = at_ref[0]
    for dz in range(nz):
        at = pl.multiple_of(lax.rem(z + dz, nz) * shard, shard)
        outs[dz][...] = turned[pl.ds(at, shard), :]


def local(features, weight, cotangent, block_values, block_coords, block_counts):
    blocks, coords = block_values[0, 0], block_coords[0, 0]
    nz, ny = lax.axis_size("row"), lax.axis_size("rep")
    nx = lax.axis_size("col") // CORES
    z, y = lax.axis_index("row"), lax.axis_index("rep")
    x, core = lax.axis_index("col") // CORES, lax.axis_index("col") % CORES
    at = jnp.stack([z, x, core, y]).astype(jnp.int32)
    count = block_counts[0]
    size = blocks.shape[1]
    rows_dev, width = cotangent.shape
    half = width // 2
    nodes, shard = features.shape
    slots = blocks.shape[0]
    flops = 2 * slots * size * size * width

    def move(a, axis, d):
        if axis == "x":
            pairs = [
                (i * CORES + c, ((i + d) % nx) * CORES + c) for i in range(nx) for c in range(CORES)
            ]
            return lax.ppermute(a, "col", pairs)
        name, n = {"y": ("rep", ny), "z": ("row", nz)}[axis]
        return lax.ppermute(a, name, [(i, (i + d) % n) for i in range(n)])

    def swap(a):
        return lax.ppermute(a, "col", [(i, i ^ 1) for i in range(nx * CORES)])

    owner = coords[:, 0] // 2
    rel_core = (owner // ny) % CORES ^ core
    rel_x = (owner // (ny * CORES) - x) % nx
    rel_y = (owner % ny - y) % ny
    pos = ((rel_core * nx + rel_x) * ny + rel_y) * 2 + coords[:, 0] % 2
    col = coords[:, 1]

    shards = [None] * nz
    shards[0] = features.T
    for k in range(1, nz // 2 + 1):
        shards[nz - k] = move(shards[(nz - k + 1) % nz], "z", 1)
        if k < nz // 2:
            shards[k] = move(shards[k - 1], "z", -1)

    part_a = shape((2, 4, rows_dev, half))
    part_b = shape((2, 3, 4, rows_dev, half))
    row_blocks = CORES * nx * ny * 2
    send_a, send_b, keep_a, keep_b = call(
        functools.partial(forward_kernel, nz, nx, ny),
        (pos, col, count, at, *shards, blocks),
        [part_a, part_b, part_a, part_b],
        [
            pltpu.VMEM((width, nodes), BF16),
            pltpu.VMEM((nodes // size, size, width), BF16),
            pltpu.VMEM((row_blocks + 1, size, width), F32),
        ],
        smem=4,
        limit=30 << 20,
        flops=flops,
    )

    recv_a, recv_b = swap(send_a), swap(send_b)
    two, four, one = shape((2, rows_dev, half)), shape((4, rows_dev, half)), shape((rows_dev, half))
    ua, ub, va, vb = call(first_sum_kernel, (keep_a, recv_a), [two] * 4)
    ua, ub, va, vb = move(ua, "x", 1), move(ub, "x", -1), move(va, "y", 1), move(vb, "y", -1)
    u1, u3, v1, v3 = call(second_sum_kernel, (keep_b, recv_b, ua, ub, va, vb), [four] * 4)
    um, up, vm, vp = move(u1, "x", 1), move(u3, "x", -1), move(v1, "y", 1), move(v3, "y", -1)
    sums = call(third_sum_kernel, (keep_b, recv_b, um, up, vm, vp), [one] * 8)
    u = [sums[0]] + [move(sums[d], "y", d) for d in (1, 2, 3)]
    v = [sums[4]] + [move(sums[4 + d], "x", d) for d in (1, 2, 3)]

    activations, back_u, back_v, w_keep, w_send = call(
        functools.partial(middle_kernel, nx, ny),
        (at, *u, *v, weight, cotangent),
        [shape((rows_dev, width)), one, one]
        + [shape((width // CORES, width), F32)] * 2,
        [pltpu.VMEM((rows_dev, width), BF16), pltpu.VMEM((width, width), F32)],
        smem=1,
    )

    tu = {0: back_u, **{(-d) % 4: move(back_u, "y", d) for d in (1, 2, 3)}}
    tv = {0: back_v, **{(-d) % 4: move(back_v, "x", d) for d in (1, 2, 3)}}
    cu, cv = call(stack_kernel, (*(tu[d] for d in range(4)), *(tv[d] for d in range(4))), [four] * 2)
    xm, xp, ym, yp = move(cu, "x", 1), move(cu, "x", -1), move(cv, "y", 1), move(cv, "y", -1)
    xl, xh, yl, yh = call(halves_kernel, (xm, xp, ym, yp), [two] * 4)
    xl, xh, yl, yh = move(xl, "x", 1), move(xh, "x", -1), move(yl, "y", 1), move(yh, "y", -1)
    mine = (cu, xm, xp, xl, xh, cv, ym, yp, yl, yh)
    theirs = tuple(swap(a) for a in mine)

    step = w_keep.shape[0] // nx
    w = (w_keep + swap(w_send)).reshape(nx, step, width)
    w = w[0] + sum(move(w[d], "x", d) for d in range(1, nx))
    w = w.reshape(ny, step // ny, width)
    w = w[0] + sum(move(w[d], "y", d) for d in range(1, ny))
    bit = 1
    while bit < nz:
        w = w + lax.ppermute(w, "row", [(i, i ^ bit) for i in range(nz)])
        bit *= 2
    w = jnp.concatenate([w] + [move(w, "y", -d) for d in range(1, ny)])
    w = jnp.concatenate([w] + [move(w, "x", -d) for d in range(1, nx)])
    (weight_grad,) = call(
        functools.partial(place_kernel, nx, ny), (at, w, swap(w)), [shape((width, width), F32)], smem=1
    )

    terms = call(
        functools.partial(backward_kernel, nz, nx, ny),
        (pos, col, count, at, *mine, *theirs, blocks),
        [shape((shard, nodes))] * nz,
        [
            pltpu.VMEM((row_blocks, size, width), BF16),
            pltpu.VMEM((nodes // size + 1, size, width), F32),
            pltpu.VMEM((width, nodes), BF16),
        ],
        smem=4,
        limit=30 << 20,
        flops=flops,
    )
    up = terms[nz // 2]
    down = terms[nz // 2 + 1]
    for k in range(nz // 2 - 1, 0, -1):
        up = added(move(up, "z", 1), terms[k])
    for k in range(nz // 2 + 2, nz):
        down = added(move(down, "z", -1), terms[k])
    input_grad = added(terms[0], move(up, "z", 1), move(down, "z", -1)).T
    return activations, input_grad, weight_grad


def solution(mesh):
    in_specs = (
        P(("col", "rep"), "row"),
        P(),
        P(("row", "col", "rep"), None),
        P("row", ("col", "rep"), None, None, None),
        P("row", ("col", "rep"), None, None),
        P("row", ("col", "rep")),
    )
    out_specs = (P(("row", "col", "rep"), None), P(("col", "rep"), "row"), P())
    return jax.shard_map(local, mesh=mesh, in_specs=in_specs, out_specs=out_specs, check_vma=False)
```

```python
import functools

import jax
import jax.numpy as jnp
from jax import lax
from jax.experimental import pallas as pl
from jax.experimental.pallas import tpu as pltpu
from jax.sharding import PartitionSpec as P

F32 = jnp.float32
BF16 = jnp.bfloat16
CORES = 2
UNROLL = 32
BIG = 44 << 20
VMEM = pl.BlockSpec(memory_space=pltpu.VMEM)
SMEM = pl.BlockSpec(memory_space=pltpu.SMEM)
HBM = pl.BlockSpec(memory_space=pltpu.HBM)


def call(kernel, args, out_shape, scratch=(), smem=0, hbm=0, limit=8 << 20, flops=0):
    moved = sum(a.size * a.dtype.itemsize for a in (*args, *out_shape))
    return pl.pallas_call(
        kernel,
        out_shape=out_shape,
        in_specs=[SMEM] * smem + [HBM] * hbm + [VMEM] * (len(args) - smem - hbm),
        out_specs=[VMEM] * len(out_shape),
        scratch_shapes=list(scratch),
        compiler_params=pltpu.CompilerParams(vmem_limit_bytes=limit),
        cost_estimate=pl.CostEstimate(flops=flops, bytes_accessed=moved, transcendentals=0),
    )(*args)


def shape(dims, dtype=BF16):
    return jax.ShapeDtypeStruct(dims, dtype)


def added(*arrays):
    total = arrays[0].astype(F32)
    for a in arrays[1:]:
        total = total + a.astype(F32)
    return total.astype(BF16)


def lanes(which, half):
    return pl.ds(pl.multiple_of(which * half, half), half)


def place(major, minor, core, block):
    return ((major * 4 + minor) * CORES + core) * 2 + block


PLACES = [(j, n, c, b) for j in range(4) for n in range(4) for c in range(CORES) for b in range(2)]


def block_copy(blocks_in, blocks, sems, t):
    part = pl.ds(t * UNROLL, UNROLL)
    return pltpu.make_async_copy(blocks_in.at[part], blocks.at[part], sems.at[t])


def forward_kernel(nz, pos_ref, col_ref, count_ref, at_ref, blocks_in, first, *refs):
    pieces, (send_a, send_b, keep_a, keep_b, blocks, turned, feat, acc, sems, first_sem) = refs[: nz - 1], refs[nz - 1 :]
    size = blocks.shape[1]
    turns = blocks.shape[0] // UNROLL
    shard = first.shape[0]
    half = acc.shape[2] // 2
    z, core = at_ref[0], at_ref[1]
    own = pltpu.make_async_copy(first, turned.at[pl.ds(pl.multiple_of(z * shard, shard), shard)], first_sem)
    own.start()
    for t in range(turns):
        block_copy(blocks_in, blocks, sems, t).start()
    rows = acc.shape[0] - 1

    def clear(r, carry):
        acc[r] = jnp.zeros(acc.shape[1:], F32)
        return carry

    lax.fori_loop(0, rows, clear, 0)
    for dz in range(1, nz):
        at = pl.multiple_of(lax.rem(z + dz, nz) * shard, shard)
        turned[pl.ds(at, shard), :] = pieces[dz - 1][...]
    own.wait()
    for c in range(feat.shape[0]):
        feat[c] = turned[:, c * size : (c + 1) * size].T
    count = count_ref[0]

    def turn(t, carry):
        block_copy(blocks_in, blocks, sems, t).wait()
        for u in range(UNROLL):
            s = t * UNROLL + u
            r = jnp.where(s < count, pos_ref[s], rows)
            acc[r] += jnp.dot(blocks[s], feat[col_ref[s]], preferred_element_type=F32)
        return carry

    lax.fori_loop(0, turns, turn, 0)
    for major, minor, c, b in PLACES:
        r = place(major, minor, c, b)
        for j, n, k, out_a, out_b, which in (
            (minor, major, 1 - c, send_a, send_b, 1 - core),
            (major, minor, c, keep_a, keep_b, core),
        ):
            value = acc[r, :, lanes(which, half)].astype(BF16)
            to = pl.ds((k * 2 + b) * size, size)
            if j == 2:
                out_a[n, to, :] = value
            else:
                out_b[(1, 3, 0).index(j), n, to, :] = value


def first_sum_kernel(keep_a, recv_a, low, high):
    low[...] = added(keep_a[:2], recv_a[:2])
    high[...] = added(keep_a[2:], recv_a[2:])


def second_sum_kernel(keep_b, recv_b, low, high, near_1, near_3):
    near_1[:2] = added(keep_b[0, :2], recv_b[0, :2], low[...])
    near_1[2:] = added(keep_b[0, 2:], recv_b[0, 2:])
    near_3[:2] = added(keep_b[1, :2], recv_b[1, :2])
    near_3[2:] = added(keep_b[1, 2:], recv_b[1, 2:], high[...])


def third_sum_kernel(keep_b, recv_b, minus, plus, *outs):
    for d in range(4):
        outs[d][...] = added(keep_b[2, d], recv_b[2, d], minus[d], plus[d])


def fourth_sum_kernel(a, b, c, d, own, send):
    rows = own.shape[0]
    own[...] = added(*(r[:rows] for r in (a, b, c, d)))
    send[...] = added(*(r[rows:] for r in (a, b, c, d)))


def weight_rows(at_ref, is_mine, step):
    core, major, minor = at_ref[1], at_ref[2], at_ref[3]
    if not is_mine:
        core, major, minor = 1 - core, minor, major
    for n in range(4):
        for j in range(4):
            chunk = (core * 4 + lax.rem(major + j, 4)) * 4 + lax.rem(minor + n, 4)
            yield pl.ds((n * 4 + j) * step, step), pl.ds(pl.multiple_of(chunk * step, step), step)


def middle_kernel(
    at_ref, own, other, weight, cotangent, act, back_own, back_send, w_keep, w_send, agg, back, terms
):
    half = own.shape[1]
    core = at_ref[1]
    agg[:, lanes(core, half)] = own[...]
    agg[:, lanes(1 - core, half)] = other[...]
    pre = jnp.dot(agg[...], weight[...], preferred_element_type=F32)
    sigma = jax.nn.sigmoid(pre)
    grad = (cotangent[...].astype(F32) * sigma * (1.0 + pre * (1.0 - sigma))).astype(BF16)
    back[...] = lax.dot_general(
        grad, weight[...], (((1,), (1,)), ((), ())), preferred_element_type=F32
    ).astype(BF16)
    back_own[...] = back[:, lanes(core, half)]
    back_send[...] = back[:, lanes(1 - core, half)]
    act[...] = (pre * sigma).astype(BF16)
    terms[...] = lax.dot_general(
        agg[...], grad, (((0,), (0,)), ((), ())), preferred_element_type=F32
    )
    step = terms.shape[0] // len(PLACES) * 2
    for out, is_mine in ((w_keep, True), (w_send, False)):
        for to, at in weight_rows(at_ref, is_mine, step):
            out[to, :] = terms[at, :]


def place_kernel(at_ref, mine, theirs, out):
    step = out.shape[0] // len(PLACES) * 2
    for piece, is_mine in ((mine, True), (theirs, False)):
        for to, at in weight_rows(at_ref, is_mine, step):
            out[at, :] = piece[to, :]


def cut(total, outs):
    rows = outs[0].shape[0]
    for d, out in enumerate(outs):
        out[...] = total[d * rows : (d + 1) * rows]


def pair_kernel(own, other, w_keep, w_recv, base, *w_outs):
    base[0] = own[...]
    base[1] = other[...]
    cut(w_keep[...] + w_recv[...], w_outs)


def line_kernel(a, b, c, d, wa, wb, wc, wd, line, *w_outs):
    for k, ref in enumerate((a, b, c, d)):
        line[k] = ref[...]
    cut(wa[...] + wb[...] + wc[...] + wd[...], w_outs)


def halves_kernel(minus, plus, wa, wb, wc, wd, low, high, w_out):
    low[...] = minus[:2]
    high[...] = plus[2:]
    w_out[...] = wa[...] + wb[...] + wc[...] + wd[...]


def ring_kernel(up, up_term, down, down_term, w, w_recv, up_out, down_out, w_out):
    up_out[...] = added(up[...], up_term[...])
    down_out[...] = added(down[...], down_term[...])
    w_out[...] = w[...] + w_recv[...]


def gather_rows(pieces, out):
    rows = pieces[0].shape[0]
    for d, piece in enumerate(pieces):
        out[d * rows : (d + 1) * rows, :] = piece[...]


def third_ring_kernel(up, up_term, down, own_term, wa, wb, wc, wd, up_out, own_out, w_out):
    up_out[...] = added(up[...], up_term[...])
    own_out[...] = down[...].astype(F32) + own_term[...].astype(F32)
    gather_rows((wa, wb, wc, wd), w_out)


def last_ring_kernel(up, own, wa, wb, wc, wd, out, w_out):
    out[...] = added(up[...], own[...])
    step = wa.shape[0] // 4
    for j, piece in enumerate((wa, wb, wc, wd)):
        for n in range(4):
            w_out[pl.ds((n * 4 + j) * step, step), :] = piece[pl.ds(n * step, step), :]


def backward_kernel(nz, pos_ref, col_ref, count_ref, at_ref, blocks_in, *refs):
    mine, theirs, (w, w_recv, w_out), outs = refs[:5], refs[5:10], refs[10:13], refs[13 : 13 + nz]
    blocks, back, acc, turned, sems = refs[13 + nz :]
    w_out[...] = w[...] + w_recv[...]
    size = blocks.shape[1]
    turns = blocks.shape[0] // UNROLL
    half = back.shape[2] // 2
    z, core = at_ref[0], at_ref[1]
    for t in range(turns):
        block_copy(blocks_in, blocks, sems, t).start()
    for (own, minus, plus, low, high), is_mine in ((mine, True), (theirs, False)):
        for major, minor, c, b in PLACES:
            source = {0: own, 3: minus, 1: plus, 2: low if minor < 2 else high}[major]
            k = minor % 2 if major == 2 else minor
            r = place(major, minor, c, b) if is_mine else place(minor, major, 1 - c, b)
            to = lanes(core if is_mine else 1 - core, half)
            back[r, :, to] = source[k, c, b * size : (b + 1) * size, :]
    cols = acc.shape[0] - 1
    for c in range(cols):
        acc[c] = jnp.zeros(acc.shape[1:], F32)
    count = count_ref[0]

    def turn(t, carry):
        block_copy(blocks_in, blocks, sems, t).wait()
        for u in range(UNROLL):
            s = t * UNROLL + u
            c = jnp.where(s < count, col_ref[s], cols)
            acc[c] += lax.dot_general(
                blocks[s], back[pos_ref[s]], (((0,), (0,)), ((), ())), preferred_element_type=F32
            )
        return carry

    lax.fori_loop(0, turns, turn, 0)
    for c in range(cols):
        turned[:, c * size : (c + 1) * size] = acc[c].astype(BF16).T
    shard = outs[0].shape[0]
    for dz in range(nz):
        at = pl.multiple_of(lax.rem(z + dz, nz) * shard, shard)
        outs[dz][...] = turned[pl.ds(at, shard), :]


def local(features, weight, cotangent, block_values, block_coords, block_counts):
    blocks, coords = block_values[0, 0], block_coords[0, 0]
    nz, ny = lax.axis_size("row"), lax.axis_size("rep")
    ncol = lax.axis_size("col")
    nx = ncol // CORES
    z, y = lax.axis_index("row"), lax.axis_index("rep")
    x, core = lax.axis_index("col") // CORES, lax.axis_index("col") % CORES
    at = jnp.stack([z, core, jnp.where(core == 0, x, y), jnp.where(core == 0, y, x)]).astype(jnp.int32)
    count = block_counts[0]
    slots, size, _ = blocks.shape
    rows_dev, width = cotangent.shape
    half = width // 2
    nodes, shard = features.shape
    flops = 2 * slots * size * size * width
    turns = slots // UNROLL

    def move(a, axis, d):
        pairs = []
        for i in range(nx):
            for c in range(CORES):
                for j in range(ny):
                    along_x = (axis == "major") == (c == 0)
                    to = ((i + d) % nx, j) if along_x else (i, (j + d) % ny)
                    pairs.append(((i * CORES + c) * ny + j, (to[0] * CORES + c) * ny + to[1]))
        return lax.ppermute(a, ("col", "rep"), pairs)

    def swap(a):
        return lax.ppermute(a, "col", [(i, i ^ 1) for i in range(ncol)])

    def along_z(a, d):
        return lax.ppermute(a, "row", [(i, (i + d) % nz) for i in range(nz)])

    def flip_z(a, bit):
        return lax.ppermute(a, "row", [(i, i ^ bit) for i in range(nz)])

    owner = coords[:, 0] // 2
    to_x = (owner // (ny * CORES) - x) % nx
    to_y = (owner % ny - y) % ny
    major, minor = jnp.where(core == 0, to_x, to_y), jnp.where(core == 0, to_y, to_x)
    pos = place(major, minor, (owner // ny) % CORES ^ core, coords[:, 0] % 2)
    col = coords[:, 1]

    shards = [None] * nz
    shards[0] = features.T
    for k in range(1, nz // 2 + 1):
        shards[nz - k] = along_z(shards[(nz - k + 1) % nz], 1)
        if k < nz // 2:
            shards[k] = along_z(shards[k - 1], -1)

    pair = CORES * rows_dev
    part_a, part_b = shape((4, pair, half)), shape((3, 4, pair, half))
    row_blocks = len(PLACES)
    send_a, send_b, keep_a, keep_b = call(
        functools.partial(forward_kernel, nz),
        (pos, col, count, at, blocks, *shards),
        [part_a, part_b, part_a, part_b],
        [
            pltpu.VMEM(blocks.shape, BF16),
            pltpu.VMEM((width, nodes), BF16),
            pltpu.VMEM((nodes // size, size, width), BF16),
            pltpu.VMEM((row_blocks + 1, size, width), F32),
            pltpu.SemaphoreType.DMA((turns,)),
            pltpu.SemaphoreType.DMA,
        ],
        smem=4,
        hbm=2,
        limit=BIG,
        flops=flops,
    )

    recv_a, recv_b = swap(send_a), swap(send_b)
    two, four, one = shape((2, pair, half)), shape((4, pair, half)), shape((pair, half))
    low, high = call(first_sum_kernel, (keep_a, recv_a), [two] * 2)
    low, high = move(low, "major", 1), move(high, "major", -1)
    near_1, near_3 = call(second_sum_kernel, (keep_b, recv_b, low, high), [four] * 2)
    minus, plus = move(near_1, "major", 1), move(near_3, "major", -1)
    sums = call(third_sum_kernel, (keep_b, recv_b, minus, plus), [one] * 4)
    sums = [sums[0]] + [move(sums[d], "minor", d) for d in (1, 2, 3)]
    mine = shape((rows_dev, half))
    agg_own, agg_send = call(fourth_sum_kernel, sums, [mine] * 2)

    w_shape = [shape((width // n, width), F32) for n in (2, 8, 32)]
    activations, back_own, back_send, w_keep, w_send = call(
        middle_kernel,
        (at, agg_own, swap(agg_send), weight, cotangent),
        [shape((rows_dev, width)), mine, mine, w_shape[0], w_shape[0]],
        [pltpu.VMEM((rows_dev, width), BF16)] * 2 + [pltpu.VMEM((width, width), F32)],
        smem=1,
    )

    base, *w = call(
        pair_kernel,
        (back_own, swap(back_send), w_keep, swap(w_send)),
        [shape((CORES, rows_dev, half))] + [w_shape[1]] * 4,
    )
    near = [base] + [move(base, "minor", -d) for d in (1, 2, 3)]
    w = [w[0]] + [move(w[d], "minor", d) for d in (1, 2, 3)]
    line, *w = call(line_kernel, (*near, *w), [shape((4, CORES, rows_dev, half))] + [w_shape[2]] * 4)
    minus, plus = move(line, "major", 1), move(line, "major", -1)
    w = [w[0]] + [move(w[d], "major", d) for d in (1, 2, 3)]
    far = shape((2, CORES, rows_dev, half))
    low, high, w = call(halves_kernel, (minus, plus, *w), [far, far, w_shape[2]])
    rows_all = (line, minus, plus, move(low, "major", 1), move(high, "major", -1))

    w, *terms = call(
        functools.partial(backward_kernel, nz),
        (pos, col, count, at, blocks, *rows_all, *(swap(a) for a in rows_all), w, flip_z(w, 1)),
        [w_shape[2]] + [shape((shard, nodes))] * nz,
        [
            pltpu.VMEM(blocks.shape, BF16),
            pltpu.VMEM((row_blocks, size, width), BF16),
            pltpu.VMEM((nodes // size + 1, size, width), F32),
            pltpu.VMEM((width, nodes), BF16),
            pltpu.SemaphoreType.DMA((turns,)),
        ],
        smem=4,
        hbm=1,
        limit=BIG,
        flops=flops,
    )
    ring = shape((shard, nodes))
    up, down = terms[4], terms[5]
    for k in (1, 2):
        up, down, w = call(
            ring_kernel,
            (along_z(up, 1), terms[4 - k], along_z(down, -1), terms[5 + k], w, flip_z(w, 2 * k)),
            [ring, ring, w_shape[2]],
        )
    w = [w] + [move(w, "minor", -d) for d in (1, 2, 3)]
    up, own, w = call(
        third_ring_kernel,
        (along_z(up, 1), terms[1], along_z(down, -1), terms[0], *w),
        [ring, shape((shard, nodes), F32), w_shape[1]],
    )
    w = [w] + [move(w, "major", -d) for d in (1, 2, 3)]
    input_grad, w = call(last_ring_kernel, (along_z(up, 1), own, *w), [ring, w_shape[0]])
    (weight_grad,) = call(place_kernel, (at, w, swap(w)), [shape((width, width), F32)], smem=1)
    return activations, input_grad.T, weight_grad


def solution(mesh):
    in_specs = (
        P(("col", "rep"), "row"),
        P(),
        P(("row", "col", "rep"), None),
        P("row", ("col", "rep"), None, None, None),
        P("row", ("col", "rep"), None, None),
        P("row", ("col", "rep")),
    )
    out_specs = (P(("row", "col", "rep"), None), P(("col", "rep"), "row"), P())
    return jax.shard_map(local, mesh=mesh, in_specs=in_specs, out_specs=out_specs, check_vma=False)
```

```python
import functools

import jax
import jax.numpy as jnp
from jax import lax
from jax.experimental import pallas as pl
from jax.experimental.pallas import tpu as pltpu
from jax.sharding import PartitionSpec as P

F32 = jnp.float32
BF16 = jnp.bfloat16
CORES = 2
UNROLL = 32
BIG = 44 << 20
VMEM = pl.BlockSpec(memory_space=pltpu.VMEM)
SMEM = pl.BlockSpec(memory_space=pltpu.SMEM)
HBM = pl.BlockSpec(memory_space=pltpu.HBM)


def call(kernel, args, out_shape, scratch=(), smem=0, hbm=0, limit=8 << 20, flops=0, aliases=None):
    moved = sum(a.size * a.dtype.itemsize for a in (*args, *out_shape))
    return pl.pallas_call(
        kernel,
        out_shape=out_shape,
        in_specs=[SMEM] * smem + [HBM] * hbm + [VMEM] * (len(args) - smem - hbm),
        out_specs=[VMEM] * len(out_shape),
        scratch_shapes=list(scratch),
        input_output_aliases=aliases or {},
        compiler_params=pltpu.CompilerParams(vmem_limit_bytes=limit),
        cost_estimate=pl.CostEstimate(flops=flops, bytes_accessed=moved, transcendentals=0),
    )(*args)


def shape(dims, dtype=BF16):
    return jax.ShapeDtypeStruct(dims, dtype)


def added(*arrays):
    total = arrays[0].astype(F32)
    for a in arrays[1:]:
        total = total + a.astype(F32)
    return total.astype(BF16)


def lanes(which, half):
    return pl.ds(pl.multiple_of(which * half, half), half)


def place(major, minor, core, block):
    return ((major * 4 + minor) * CORES + core) * 2 + block


PLACES = [(j, n, c, b) for j in range(4) for n in range(4) for c in range(CORES) for b in range(2)]


def block_copy(blocks_in, blocks, sems, t):
    part = pl.ds(t * UNROLL, UNROLL)
    return pltpu.make_async_copy(blocks_in.at[part], blocks.at[part], sems.at[t])


def forward_kernel(nz, pos_ref, col_ref, count_ref, at_ref, blocks_in, first, *refs):
    pieces, (send_a, send_b, keep_a, keep_b, blocks, turned, feat, acc, sems, first_sem) = refs[: nz - 1], refs[nz - 1 :]
    size = blocks.shape[1]
    turns = blocks.shape[0] // UNROLL
    shard = first.shape[0]
    half = acc.shape[2] // 2
    z, core = at_ref[0], at_ref[1]
    own = pltpu.make_async_copy(first, turned.at[pl.ds(pl.multiple_of(z * shard, shard), shard)], first_sem)
    own.start()
    for t in range(turns):
        block_copy(blocks_in, blocks, sems, t).start()
    rows = acc.shape[0] - 1

    def clear(r, carry):
        acc[r] = jnp.zeros(acc.shape[1:], F32)
        return carry

    lax.fori_loop(0, rows, clear, 0)
    for dz in range(1, nz):
        at = pl.multiple_of(lax.rem(z + dz, nz) * shard, shard)
        turned[pl.ds(at, shard), :] = pieces[dz - 1][...]
    own.wait()
    for c in range(feat.shape[0]):
        feat[c] = turned[:, c * size : (c + 1) * size].T
    count = count_ref[0]

    def turn(t, carry):
        block_copy(blocks_in, blocks, sems, t).wait()
        for u in range(UNROLL):
            s = t * UNROLL + u
            r = jnp.where(s < count, pos_ref[s], rows)
            acc[r] += jnp.dot(blocks[s], feat[col_ref[s]], preferred_element_type=F32)
        return carry

    lax.fori_loop(0, turns, turn, 0)
    for major, minor, c, b in PLACES:
        r = place(major, minor, c, b)
        for j, n, k, out_a, out_b, which in (
            (minor, major, 1 - c, send_a, send_b, 1 - core),
            (major, minor, c, keep_a, keep_b, core),
        ):
            value = acc[r, :, lanes(which, half)].astype(BF16)
            to = pl.ds((k * 2 + b) * size, size)
            if j == 2:
                out_a[n, to, :] = value
            else:
                out_b[(1, 3, 0).index(j), n, to, :] = value


def first_sum_kernel(keep_a, recv_a, passed_in, low, high, passed):
    low[...] = added(keep_a[:2], recv_a[:2])
    high[...] = added(keep_a[2:], recv_a[2:])


def second_sum_kernel(keep_b, recv_b, low, high, near_1, near_3):
    near_1[:2] = added(keep_b[0, :2], recv_b[0, :2], low[...])
    near_1[2:] = added(keep_b[0, 2:], recv_b[0, 2:])
    near_3[:2] = added(keep_b[1, :2], recv_b[1, :2])
    near_3[2:] = added(keep_b[1, 2:], recv_b[1, 2:], high[...])


def third_sum_kernel(keep_b, recv_b, minus, plus, *outs):
    for d in range(4):
        outs[d][...] = added(keep_b[2, d], recv_b[2, d], minus[d], plus[d])


def fourth_sum_kernel(a, b, c, d, own, send):
    rows = own.shape[0]
    own[...] = added(*(r[:rows] for r in (a, b, c, d)))
    send[...] = added(*(r[rows:] for r in (a, b, c, d)))


def middle_kernel(at_ref, own, other, weight, cotangent, act, back_own, send, w_keep, agg, back, terms):
    rows, half = own.shape
    core = at_ref[1]
    agg[:, lanes(core, half)] = own[...]
    agg[:, lanes(1 - core, half)] = other[...]
    pre = jnp.dot(agg[...], weight[...], preferred_element_type=F32)
    sigma = jax.nn.sigmoid(pre)
    grad = (cotangent[...].astype(F32) * sigma * (1.0 + pre * (1.0 - sigma))).astype(BF16)
    back[...] = lax.dot_general(
        grad, weight[...], (((1,), (1,)), ((), ())), preferred_element_type=F32
    ).astype(BF16)
    back_own[...] = back[:, lanes(core, half)]
    send[:rows, :] = back[:, lanes(1 - core, half)]
    act[...] = (pre * sigma).astype(BF16)
    terms[...] = lax.dot_general(
        agg[...], grad, (((0,), (0,)), ((), ())), preferred_element_type=F32
    )
    for k in range(2):
        columns = slice(k * half, (k + 1) * half)
        w_keep[k * half : (k + 1) * half, :] = terms[lanes(core, half), columns]
        send[rows + k * half : rows + (k + 1) * half, :] = terms[lanes(1 - core, half), columns].astype(BF16)


def in_order(table, first, *pieces):
    n = len(pieces)
    for d, piece in enumerate(pieces):
        table[lax.rem(first + d, n)] = piece.astype(F32)
    total = table[0]
    for d in range(1, n):
        total = total + table[d]
    return total


def pair_kernel(own, recv, w_keep, out):
    rows = own.shape[0]
    out[:rows, :] = own[...]
    out[rows : 2 * rows, :] = recv[:rows]
    out[2 * rows :, :] = added(w_keep[...], recv[rows:])


def line_kernel(at_ref, a, b, c, d, out, table):
    rows = table.shape[1] * 2
    for k, ref in enumerate((a, b, c, d)):
        out[k * rows : (k + 1) * rows, :] = ref[:rows]
    out[4 * rows :, :] = in_order(table, at_ref[3], *(ref[rows:] for ref in (a, b, c, d))).astype(BF16)


def halves_kernel(minus, plus, low, high):
    rows = high.shape[0]
    low[:rows, :] = minus[:rows]
    low[rows:, :] = minus[2 * rows :]
    high[...] = plus[rows : 2 * rows]


def plane_kernel(at_ref, own, plus, low, minus, out, table):
    rows = out.shape[0]
    out[...] = in_order(table, at_ref[2], *(ref[ref.shape[0] - rows :] for ref in (own, plus, low, minus))).astype(BF16)


def first_ring_kernel(up, up_term, down, down_term, w, w_recv, up_out, down_out):
    rows = up.shape[0]
    up_out[:rows, :] = added(up[...], up_term[...])
    down_out[:rows, :] = added(down[...], down_term[...])
    both = added(w[...], w_recv[...])
    up_out[rows:, :] = both
    down_out[rows:, :] = both


def second_ring_kernel(up, up_term, down, down_term, up_out, down_out):
    rows = up_term.shape[0]
    up_out[:rows, :] = added(up[:rows], up_term[...])
    up_out[rows:, :] = up[rows:]
    down_out[...] = added(down[:rows], down_term[...])


def third_ring_kernel(at_ref, up, up_term, down, own_term, w, w_plus, w_minus, up_out, own_out, w_out, table):
    rows = up_term.shape[0]
    up_out[...] = added(up[:rows], up_term[...])
    own_out[...] = down[...].astype(F32) + own_term[...].astype(F32)
    w_out[...] = in_order(table, lax.rem(at_ref[0], 4), *(ref[rows:] for ref in (w, w_plus, up, w_minus)))


def last_ring_kernel(at_ref, up, own, w, w_recv, out, w_out):
    total = added(up[...], own[...])
    width = total.shape[1]
    for c in range(out.shape[1] // width):
        out[:, c * width : (c + 1) * width] = total[c * out.shape[0] : (c + 1) * out.shape[0]]
    core, half = at_ref[1], w_out.shape[0] // 2
    for which, piece in ((core, w), (1 - core, w_recv)):
        for k in range(2):
            w_out[lanes(which, half), k * half : (k + 1) * half] = piece[k * half : (k + 1) * half]


def backward_kernel(nz, pos_ref, col_ref, count_ref, at_ref, blocks_in, *refs):
    mine, theirs, outs = refs[:5], refs[5:10], refs[10 : 10 + nz]
    blocks, back, acc, turned, sems = refs[10 + nz :]
    size = blocks.shape[1]
    turns = blocks.shape[0] // UNROLL
    half = back.shape[2] // 2
    z, core = at_ref[0], at_ref[1]
    for t in range(turns):
        block_copy(blocks_in, blocks, sems, t).start()
    for (own, minus, plus, low, high), is_mine in ((mine, True), (theirs, False)):
        for major, minor, c, b in PLACES:
            source = {0: own, 3: minus, 1: plus, 2: low if minor < 2 else high}[major]
            k = minor % 2 if major == 2 else minor
            k = ((k * CORES + c) * 2 + b) * size
            r = place(major, minor, c, b) if is_mine else place(minor, major, 1 - c, b)
            to = lanes(core if is_mine else 1 - core, half)
            back[r, :, to] = source[k : k + size, :]
    cols = acc.shape[0] - 1
    for c in range(cols):
        acc[c] = jnp.zeros(acc.shape[1:], F32)
    count = count_ref[0]

    def turn(t, carry):
        block_copy(blocks_in, blocks, sems, t).wait()
        for u in range(UNROLL):
            s = t * UNROLL + u
            c = jnp.where(s < count, col_ref[s], cols)
            acc[c] += lax.dot_general(
                blocks[s], back[pos_ref[s]], (((0,), (0,)), ((), ())), preferred_element_type=F32
            )
        return carry

    lax.fori_loop(0, turns, turn, 0)
    shard = turned.shape[1] // nz
    for c in range(cols):
        turned[c] = acc[c].astype(BF16).T
        for dz in range(nz):
            at = pl.multiple_of(lax.rem(z + dz, nz) * shard, shard)
            outs[dz][c * shard : (c + 1) * shard, :] = turned[c, pl.ds(at, shard), :]


def local(features, weight, cotangent, block_values, block_coords, block_counts):
    blocks, coords = block_values[0, 0], block_coords[0, 0]
    nz, ny = lax.axis_size("row"), lax.axis_size("rep")
    ncol = lax.axis_size("col")
    nx = ncol // CORES
    z, y = lax.axis_index("row"), lax.axis_index("rep")
    x, core = lax.axis_index("col") // CORES, lax.axis_index("col") % CORES
    at = jnp.stack([z, core, jnp.where(core == 0, x, y), jnp.where(core == 0, y, x)]).astype(jnp.int32)
    count = block_counts[0]
    slots, size, _ = blocks.shape
    rows_dev, width = cotangent.shape
    half = width // 2
    nodes, shard = features.shape
    flops = 2 * slots * size * size * width
    turns = slots // UNROLL

    def move(a, axis, d):
        pairs = []
        for i in range(nx):
            for c in range(CORES):
                for j in range(ny):
                    along_x = (axis == "major") == (c == 0)
                    to = ((i + d) % nx, j) if along_x else (i, (j + d) % ny)
                    pairs.append(((i * CORES + c) * ny + j, (to[0] * CORES + c) * ny + to[1]))
        return lax.ppermute(a, ("col", "rep"), pairs)

    def swap(a):
        return lax.ppermute(a, "col", [(i, i ^ 1) for i in range(ncol)])

    def along_z(a, d):
        return lax.ppermute(a, "row", [(i, (i + d) % nz) for i in range(nz)])

    def flip_z(a, bit):
        return lax.ppermute(a, "row", [(i, i ^ bit) for i in range(nz)])

    owner = coords[:, 0] // 2
    to_x = (owner // (ny * CORES) - x) % nx
    to_y = (owner % ny - y) % ny
    major, minor = jnp.where(core == 0, to_x, to_y), jnp.where(core == 0, to_y, to_x)
    pos = place(major, minor, (owner // ny) % CORES ^ core, coords[:, 0] % 2)
    col = coords[:, 1]

    shards = [None] * nz
    shards[0] = features.T
    for k in range(1, nz // 2 + 1):
        shards[nz - k] = along_z(shards[(nz - k + 1) % nz], 1)
        if k < nz // 2:
            shards[k] = along_z(shards[k - 1], -1)

    pair = CORES * rows_dev
    part_a, part_b = shape((4, pair, half)), shape((3, 4, pair, half))
    row_blocks = len(PLACES)
    send_a, send_b, keep_a, keep_b = call(
        functools.partial(forward_kernel, nz),
        (pos, col, count, at, blocks, *shards),
        [part_a, part_b, part_a, part_b],
        [
            pltpu.VMEM(blocks.shape, BF16),
            pltpu.VMEM((width, nodes), BF16),
            pltpu.VMEM((nodes // size, size, width), BF16),
            pltpu.VMEM((row_blocks + 1, size, width), F32),
            pltpu.SemaphoreType.DMA((turns,)),
            pltpu.SemaphoreType.DMA,
        ],
        smem=4,
        hbm=2,
        limit=BIG,
        flops=flops,
    )

    recv_a = swap(send_a)
    two, four, one = shape((2, pair, half)), shape((4, pair, half)), shape((pair, half))
    low, high, send_b = call(first_sum_kernel, (keep_a, recv_a, send_b), [two, two, part_b], aliases={2: 2})
    low, high, recv_b = move(low, "major", 1), move(high, "major", -1), swap(send_b)
    near_1, near_3 = call(second_sum_kernel, (keep_b, recv_b, low, high), [four] * 2)
    minus, plus = move(near_1, "major", 1), move(near_3, "major", -1)
    sums = call(third_sum_kernel, (keep_b, recv_b, minus, plus), [one] * 4)
    sums = [sums[0]] + [move(sums[d], "minor", d) for d in (1, 2, 3)]
    mine = shape((rows_dev, half))
    agg_own, agg_send = call(fourth_sum_kernel, sums, [mine] * 2)

    w_half = shape((width, half))
    activations, back_own, send, w_keep = call(
        middle_kernel,
        (at, agg_own, swap(agg_send), weight, cotangent),
        [shape((rows_dev, width)), mine, shape((rows_dev + width, half)), shape((width, half), F32)],
        [pltpu.VMEM((rows_dev, width), BF16)] * 2 + [pltpu.VMEM((width, width), F32)],
        smem=1,
    )
    table = pltpu.VMEM((4, width, half), F32)

    (base,) = call(pair_kernel, (back_own, swap(send), w_keep), [shape((pair + width, half))])
    near = [base] + [move(base, "minor", -d) for d in (1, 2, 3)]
    (line,) = call(line_kernel, (at, *near), [shape((4 * pair + width, half))], [table], smem=1)
    minus, plus = move(line, "major", 1), move(line, "major", -1)
    low, high = call(halves_kernel, (minus, plus), [shape((2 * pair + width, half)), shape((2 * pair, half))])
    low, high = move(low, "major", 1), move(high, "major", -1)
    rows_all = (line, minus, plus, low, high)
    (w,) = call(plane_kernel, (at, line, plus, low, minus), [w_half], [table], smem=1)

    ring, ring_w = shape((shard * nodes // size, size)), shape((shard * nodes // size + width, half))
    w_recv = flip_z(w, 4)
    terms = call(
        functools.partial(backward_kernel, nz),
        (pos, col, count, at, blocks, *rows_all, *(swap(a) for a in rows_all)),
        [ring] * nz,
        [
            pltpu.VMEM(blocks.shape, BF16),
            pltpu.VMEM((row_blocks, size, width), BF16),
            pltpu.VMEM((nodes // size + 1, size, width), F32),
            pltpu.VMEM((nodes // size, width, size), BF16),
            pltpu.SemaphoreType.DMA((turns,)),
        ],
        smem=4,
        hbm=1,
        limit=BIG,
        flops=flops,
    )
    up, down = along_z(terms[4], 1), along_z(terms[5], -1)
    own, down = call(first_ring_kernel, (up, terms[3], down, terms[6], w, w_recv), [ring_w] * 2)
    up, down = along_z(own, 1), along_z(down, -1)
    next_up, next_down = call(second_ring_kernel, (up, terms[2], down, terms[7]), [ring_w, ring])
    third_up, third_down = along_z(next_up, 1), along_z(next_down, -1)
    up, own, w = call(
        third_ring_kernel,
        (at, third_up, terms[1], third_down, terms[0], own, down, up),
        [ring, shape(ring.shape, F32), shape((width, half), F32)],
        [table],
        smem=1,
    )
    input_grad, weight_grad = call(
        last_ring_kernel,
        (at, along_z(up, 1), own, w, swap(w)),
        [shape((shard, nodes)), shape((width, width), F32)],
        smem=1,
    )
    return activations, input_grad.T, weight_grad


def solution(mesh):
    in_specs = (
        P(("col", "rep"), "row"),
        P(),
        P(("row", "col", "rep"), None),
        P("row", ("col", "rep"), None, None, None),
        P("row", ("col", "rep"), None, None),
        P("row", ("col", "rep")),
    )
    out_specs = (P(("row", "col", "rep"), None), P(("col", "rep"), "row"), P())
    return jax.shard_map(local, mesh=mesh, in_specs=in_specs, out_specs=out_specs, check_vma=False)
```

```python
import functools

import jax
import jax.numpy as jnp
from jax import lax
from jax.experimental import pallas as pl
from jax.experimental.pallas import tpu as pltpu
from jax.sharding import PartitionSpec as P

F32 = jnp.float32
BF16 = jnp.bfloat16
CORES = 2
UNROLL = 64
BIG = 44 << 20
VMEM = pl.BlockSpec(memory_space=pltpu.VMEM)
SMEM = pl.BlockSpec(memory_space=pltpu.SMEM)
HBM = pl.BlockSpec(memory_space=pltpu.HBM)


def call(kernel, args, out_shape, scratch=(), smem=0, hbm=0, limit=8 << 20, flops=0, aliases=None):
    moved = sum(a.size * a.dtype.itemsize for a in (*args, *out_shape))
    return pl.pallas_call(
        kernel,
        out_shape=out_shape,
        in_specs=[SMEM] * smem + [HBM] * hbm + [VMEM] * (len(args) - smem - hbm),
        out_specs=[VMEM] * len(out_shape),
        scratch_shapes=list(scratch),
        input_output_aliases=aliases or {},
        compiler_params=pltpu.CompilerParams(vmem_limit_bytes=limit),
        cost_estimate=pl.CostEstimate(flops=flops, bytes_accessed=moved, transcendentals=0),
    )(*args)


def shape(dims, dtype=BF16):
    return jax.ShapeDtypeStruct(dims, dtype)


def added(*arrays):
    total = arrays[0].astype(F32)
    for a in arrays[1:]:
        total = total + a.astype(F32)
    return total.astype(BF16)


def lanes(which, half):
    return pl.ds(pl.multiple_of(which * half, half), half)


def place(major, minor, core, block):
    return ((major * 4 + minor) * CORES + core) * 2 + block


PLACES = [(j, n, c, b) for j in range(4) for n in range(4) for c in range(CORES) for b in range(2)]


def row_place(coord_ref, at_ref, s):
    r = coord_ref[0, s]
    core, axes = at_ref[1], (at_ref[2], at_ref[3])
    along_x, along_y = jnp.right_shift(r, 4), jnp.bitwise_and(jnp.right_shift(r, 1), 3)
    major = jnp.bitwise_and(jnp.where(core == 0, along_x, along_y) - axes[0], 3)
    minor = jnp.bitwise_and(jnp.where(core == 0, along_y, along_x) - axes[1], 3)
    own = jnp.bitwise_xor(jnp.bitwise_and(jnp.right_shift(r, 3), 1), core)
    return place(major, minor, own, jnp.bitwise_and(r, 1))


def own_kernel(first, out, sem):
    copy = pltpu.make_async_copy(first, out, sem)
    copy.start()
    copy.wait()


def block_copy(blocks_in, blocks, sems, t):
    part = pl.ds(t * UNROLL, UNROLL)
    return pltpu.make_async_copy(blocks_in.at[part], blocks.at[part], sems.at[t])


def forward_kernel(nz, coord_ref, count_ref, at_ref, blocks_in, *refs):
    pieces, (send_a, send_b, keep_a, keep_b, blocks, turned, feat, acc, sems) = refs[:nz], refs[nz:]
    size = blocks.shape[1]
    turns = blocks.shape[0] // UNROLL
    shard = pieces[0].shape[0]
    half = acc.shape[2] // 2
    z, core = at_ref[0], at_ref[1]
    for t in range(turns):
        block_copy(blocks_in, blocks, sems, t).start()
    rows = acc.shape[0] - 1

    def clear(r, carry):
        acc[r] = jnp.zeros(acc.shape[1:], F32)
        return carry

    lax.fori_loop(0, rows, clear, 0)
    for dz in range(nz):
        at = pl.multiple_of(lax.rem(z + dz, nz) * shard, shard)
        turned[pl.ds(at, shard), :] = pieces[dz][...]
    for c in range(feat.shape[0]):
        feat[c] = turned[:, c * size : (c + 1) * size].T
    count = count_ref[0]

    def turn(t, carry):
        block_copy(blocks_in, blocks, sems, t).wait()
        for u in range(UNROLL):
            s = t * UNROLL + u
            r = jnp.where(s < count, row_place(coord_ref, at_ref, s), rows)
            acc[r] += jnp.dot(blocks[s], feat[coord_ref[1, s]], preferred_element_type=F32)
        return carry

    lax.fori_loop(0, turns, turn, 0)
    for major, minor, c, b in PLACES:
        r = place(major, minor, c, b)
        for j, n, k, out_a, out_b, which in (
            (minor, major, 1 - c, send_a, send_b, 1 - core),
            (major, minor, c, keep_a, keep_b, core),
        ):
            value = acc[r, :, lanes(which, half)].astype(BF16)
            to = pl.ds((k * 2 + b) * size, size)
            if j == 2:
                out_a[n, to, :] = value
            else:
                out_b[(1, 3, 0).index(j), n, to, :] = value


def first_sum_kernel(keep_a, recv_a, passed_in, low, high, passed):
    low[...] = added(keep_a[:2], recv_a[:2])
    high[...] = added(keep_a[2:], recv_a[2:])


def second_sum_kernel(keep_b, recv_b, low, high, near_1, near_3):
    near_1[:2] = added(keep_b[0, :2], recv_b[0, :2], low[...])
    near_1[2:] = added(keep_b[0, 2:], recv_b[0, 2:])
    near_3[:2] = added(keep_b[1, :2], recv_b[1, :2])
    near_3[2:] = added(keep_b[1, 2:], recv_b[1, 2:], high[...])


def third_sum_kernel(keep_b, recv_b, minus, plus, *outs):
    for d in range(4):
        outs[d][...] = added(keep_b[2, d], recv_b[2, d], minus[d], plus[d])


def fourth_sum_kernel(a, b, c, d, own, send):
    rows = own.shape[0]
    own[...] = added(*(r[:rows] for r in (a, b, c, d)))
    send[...] = added(*(r[rows:] for r in (a, b, c, d)))


def middle_kernel(at_ref, own, other, weight, cotangent, act, back_own, send, w_keep, agg, back, terms):
    rows, half = own.shape
    core = at_ref[1]
    agg[:, lanes(core, half)] = own[...]
    agg[:, lanes(1 - core, half)] = other[...]
    pre = jnp.dot(agg[...], weight[...], preferred_element_type=F32)
    sigma = jax.nn.sigmoid(pre)
    grad = (cotangent[...].astype(F32) * sigma * (1.0 + pre * (1.0 - sigma))).astype(BF16)
    back[...] = lax.dot_general(
        grad, weight[...], (((1,), (1,)), ((), ())), preferred_element_type=F32
    ).astype(BF16)
    back_own[...] = back[:, lanes(core, half)]
    send[:rows, :] = back[:, lanes(1 - core, half)]
    act[...] = (pre * sigma).astype(BF16)
    terms[...] = lax.dot_general(
        agg[...], grad, (((0,), (0,)), ((), ())), preferred_element_type=F32
    )
    for k in range(2):
        columns = slice(k * half, (k + 1) * half)
        w_keep[k * half : (k + 1) * half, :] = terms[lanes(core, half), columns]
        send[rows + k * half : rows + (k + 1) * half, :] = terms[lanes(1 - core, half), columns].astype(BF16)


def in_order(table, first, *pieces):
    n = len(pieces)
    for d, piece in enumerate(pieces):
        table[lax.rem(first + d, n)] = piece.astype(F32)
    total = table[0]
    for d in range(1, n):
        total = total + table[d]
    return total


def pair_kernel(own, recv, w_keep, out):
    rows = own.shape[0]
    out[:rows, :] = own[...]
    out[rows : 2 * rows, :] = recv[:rows]
    out[2 * rows :, :] = added(w_keep[...], recv[rows:])


def line_kernel(at_ref, a, b, c, d, out, table):
    rows = table.shape[1] * 2
    for k, ref in enumerate((a, b, c, d)):
        out[k * rows : (k + 1) * rows, :] = ref[:rows]
    out[4 * rows :, :] = in_order(table, at_ref[3], *(ref[rows:] for ref in (a, b, c, d))).astype(BF16)


def halves_kernel(minus, plus, passed_in, low, high, between, passed):
    rows = high.shape[0]
    low[:rows, :] = minus[:rows]
    low[rows:, :] = minus[2 * rows :]
    high[...] = plus[rows : 2 * rows]
    between[: 2 * rows, :] = minus[: 2 * rows]
    between[2 * rows :, :] = plus[: 2 * rows]


def ring_kernel(up, up_term, down, down_term, up_out, down_out):
    rows = up_term.shape[0]
    for got, term, out in ((up, up_term, up_out), (down, down_term, down_out)):
        out[:rows, :] = added(got[:rows], term[...])
        out[rows:, :] = got[rows:]


def third_ring_kernel(at_ref, up, up_term, down, own_term, *refs):
    w, opposite, up_1, down_1, up_2, down_2, up_out, own_out, w_out, table = refs
    rows = up_term.shape[0]
    up_out[...] = added(up[:rows], up_term[...])
    own_out[...] = down[:rows].astype(F32) + own_term[...].astype(F32)
    tails = (ref[rows:] for ref in (down_1, down_2, down))
    after = (ref[rows:] for ref in (up, up_2, up_1))
    w_out[...] = in_order(table, at_ref[0], w[...], *tails, opposite[...], *after)


def last_ring_kernel(at_ref, up, own, w, w_recv, out, w_out):
    total = added(up[...], own[...])
    width = total.shape[1]
    for c in range(out.shape[1] // width):
        out[:, c * width : (c + 1) * width] = total[c * out.shape[0] : (c + 1) * out.shape[0]]
    core, half = at_ref[1], w_out.shape[0] // 2
    for which, piece in ((core, w), (1 - core, w_recv)):
        for k in range(2):
            w_out[lanes(which, half), k * half : (k + 1) * half] = piece[k * half : (k + 1) * half]


def backward_kernel(nz, coord_ref, count_ref, at_ref, blocks_in, *refs):
    mine, (line, between, low, high), (w, *outs) = refs[:5], refs[5:9], refs[9 : 10 + nz]
    blocks, back, acc, turned, table, sems = refs[10 + nz :]
    rows = between.shape[0] // 2
    theirs = (line, between.at[:rows], between.at[rows:], low, high)
    size = blocks.shape[1]
    turns = blocks.shape[0] // UNROLL
    half = back.shape[2] // 2
    z, core = at_ref[0], at_ref[1]
    for t in range(turns):
        block_copy(blocks_in, blocks, sems, t).start()
    for (own, minus, plus, low, high), is_mine in ((mine, True), (theirs, False)):
        for major, minor, c, b in PLACES:
            source = {0: own, 3: minus, 1: plus, 2: low if minor < 2 else high}[major]
            k = minor % 2 if major == 2 else minor
            k = ((k * CORES + c) * 2 + b) * size
            r = place(major, minor, c, b) if is_mine else place(minor, major, 1 - c, b)
            to = lanes(core if is_mine else 1 - core, half)
            back[r, :, to] = source[k : k + size, :]
    cols = acc.shape[0] - 1
    for c in range(cols):
        acc[c] = jnp.zeros(acc.shape[1:], F32)
    count = count_ref[0]

    def turn(t, carry):
        block_copy(blocks_in, blocks, sems, t).wait()
        for u in range(UNROLL):
            s = t * UNROLL + u
            c = jnp.where(s < count, coord_ref[1, s], cols)
            acc[c] += lax.dot_general(
                blocks[s], back[row_place(coord_ref, at_ref, s)], (((0,), (0,)), ((), ())), preferred_element_type=F32
            )
        return carry

    lax.fori_loop(0, turns, turn, 0)
    own, minus, plus, low, high = mine
    rows = w.shape[0]
    tails = (ref[ref.shape[0] - rows :] for ref in (own, plus, low, minus))
    w[...] = in_order(table, at_ref[2], *tails).astype(BF16)
    for out in (outs[4], outs[5]):
        out[out.shape[0] - rows :, :] = w[...]
    shard = turned.shape[1] // nz
    for c in range(cols):
        turned[c] = acc[c].astype(BF16).T
        for dz in range(nz):
            at = pl.multiple_of(lax.rem(z + dz, nz) * shard, shard)
            outs[dz][c * shard : (c + 1) * shard, :] = turned[c, pl.ds(at, shard), :]


def local(features, weight, cotangent, block_values, block_coords, block_counts):
    blocks, coords = block_values[0, 0], block_coords[0, 0]
    nz, ny = lax.axis_size("row"), lax.axis_size("rep")
    ncol = lax.axis_size("col")
    nx = ncol // CORES
    z, y = lax.axis_index("row"), lax.axis_index("rep")
    x, core = lax.axis_index("col") // CORES, lax.axis_index("col") % CORES
    at = jnp.stack([z, core, jnp.where(core == 0, x, y), jnp.where(core == 0, y, x)]).astype(jnp.int32)
    count = block_counts[0]
    coords = coords.T
    slots, size, _ = blocks.shape
    rows_dev, width = cotangent.shape
    half = width // 2
    nodes, shard = features.shape
    flops = 2 * slots * size * size * width
    turns = slots // UNROLL

    def move(a, axis, d):
        pairs = []
        for i in range(nx):
            for c in range(CORES):
                for j in range(ny):
                    along_x = (axis == "major") == (c == 0)
                    to = ((i + d) % nx, j) if along_x else (i, (j + d) % ny)
                    pairs.append(((i * CORES + c) * ny + j, (to[0] * CORES + c) * ny + to[1]))
        return lax.ppermute(a, ("col", "rep"), pairs)

    def swap(a):
        return lax.ppermute(a, "col", [(i, i ^ 1) for i in range(ncol)])

    def along_z(a, d):
        return lax.ppermute(a, "row", [(i, (i + d) % nz) for i in range(nz)])

    def flip_z(a, bit):
        return lax.ppermute(a, "row", [(i, i ^ bit) for i in range(nz)])

    shards = [None] * nz
    shards[0] = features.T
    for k in range(1, nz // 2 + 1):
        shards[nz - k] = along_z(shards[(nz - k + 1) % nz], 1)
        if k < nz // 2:
            shards[k] = along_z(shards[k - 1], -1)

    (shards[0],) = call(
        own_kernel, (shards[0],), [shape((shard, nodes))], [pltpu.SemaphoreType.DMA], hbm=1
    )
    pair = CORES * rows_dev
    part_a, part_b = shape((4, pair, half)), shape((3, 4, pair, half))
    row_blocks = len(PLACES)
    send_a, send_b, keep_a, keep_b = call(
        functools.partial(forward_kernel, nz),
        (coords, count, at, blocks, *shards),
        [part_a, part_b, part_a, part_b],
        [
            pltpu.VMEM(blocks.shape, BF16),
            pltpu.VMEM((width, nodes), BF16),
            pltpu.VMEM((nodes // size, size, width), BF16),
            pltpu.VMEM((row_blocks + 1, size, width), F32),
            pltpu.SemaphoreType.DMA((turns,)),
        ],
        smem=3,
        hbm=1,
        limit=BIG,
        flops=flops,
    )

    recv_a = swap(send_a)
    two, four, one = shape((2, pair, half)), shape((4, pair, half)), shape((pair, half))
    low, high, send_b = call(first_sum_kernel, (keep_a, recv_a, send_b), [two, two, part_b], aliases={2: 2})
    low, high, recv_b = move(low, "major", 1), move(high, "major", -1), swap(send_b)
    near_1, near_3 = call(second_sum_kernel, (keep_b, recv_b, low, high), [four] * 2)
    minus, plus = move(near_1, "major", 1), move(near_3, "major", -1)
    sums = call(third_sum_kernel, (keep_b, recv_b, minus, plus), [one] * 4)
    sums = [sums[0]] + [move(sums[d], "minor", d) for d in (1, 2, 3)]
    mine = shape((rows_dev, half))
    agg_own, agg_send = call(fourth_sum_kernel, sums, [mine] * 2)

    w_half = shape((width, half))
    activations, back_own, send, w_keep = call(
        middle_kernel,
        (at, agg_own, swap(agg_send), weight, cotangent),
        [shape((rows_dev, width)), mine, shape((rows_dev + width, half)), shape((width, half), F32)],
        [pltpu.VMEM((rows_dev, width), BF16)] * 2 + [pltpu.VMEM((width, width), F32)],
        smem=1,
    )
    table = pltpu.VMEM((4, width, half), F32)

    (base,) = call(pair_kernel, (back_own, swap(send), w_keep), [shape((pair + width, half))])
    near = [base] + [move(base, "minor", -d) for d in (1, 2, 3)]
    (line,) = call(line_kernel, (at, *near), [shape((4 * pair + width, half))], [table], smem=1)
    minus, plus = move(line, "major", 1), move(line, "major", -1)
    sibling_line = swap(line)
    low, high, between, sibling_line = call(
        halves_kernel,
        (minus, plus, sibling_line),
        [
            shape((2 * pair + width, half)),
            shape((2 * pair, half)),
            shape((8 * pair, half)),
            shape(line.shape),
        ],
        aliases={2: 3},
    )
    low, high, between = move(low, "major", 1), move(high, "major", -1), swap(between)
    rows_all = (line, minus, plus, low, high, sibling_line, between, swap(low), swap(high))

    cells = shard * nodes // size
    ring, ring_w = shape((cells, size)), shape((cells + width, size))
    w, *terms = call(
        functools.partial(backward_kernel, nz),
        (coords, count, at, blocks, *rows_all),
        [w_half] + [ring_w if k in (4, 5) else ring for k in range(nz)],
        [
            pltpu.VMEM(blocks.shape, BF16),
            pltpu.VMEM((row_blocks, size, width), BF16),
            pltpu.VMEM((nodes // size + 1, size, width), F32),
            pltpu.VMEM((nodes // size, width, size), BF16),
            table,
            pltpu.SemaphoreType.DMA((turns,)),
        ],
        smem=3,
        hbm=1,
        limit=BIG,
        flops=flops,
    )
    up_1, down_1 = along_z(terms[4], 1), along_z(terms[5], -1)
    up, down = call(ring_kernel, (up_1, terms[3], down_1, terms[6]), [ring_w] * 2)
    up_2, down_2 = along_z(up, 1), along_z(down, -1)
    up, down = call(ring_kernel, (up_2, terms[2], down_2, terms[7]), [ring_w] * 2)
    up_3, down_3 = along_z(up, 1), along_z(down, -1)
    up, own, w = call(
        third_ring_kernel,
        (at, up_3, terms[1], down_3, terms[0], w, flip_z(w, 4), up_1, down_1, up_2, down_2),
        [ring, shape((cells, size), F32), shape((width, half), F32)],
        [pltpu.VMEM((nz, width, half), F32)],
        smem=1,
    )
    input_grad, weight_grad = call(
        last_ring_kernel,
        (at, along_z(up, 1), own, w, swap(w)),
        [shape((shard, nodes)), shape((width, width), F32)],
        smem=1,
    )
    return activations, input_grad.T, weight_grad


def solution(mesh):
    in_specs = (
        P(("col", "rep"), "row"),
        P(),
        P(("row", "col", "rep"), None),
        P("row", ("col", "rep"), None, None, None),
        P("row", ("col", "rep"), None, None),
        P("row", ("col", "rep")),
    )
    out_specs = (P(("row", "col", "rep"), None), P(("col", "rep"), "row"), P())
    return jax.shard_map(local, mesh=mesh, in_specs=in_specs, out_specs=out_specs, check_vma=False)
```

```python
import functools

import jax
import jax.numpy as jnp
from jax import lax
from jax.experimental import pallas as pl
from jax.experimental.pallas import tpu as pltpu
from jax.sharding import PartitionSpec as P

F32 = jnp.float32
BF16 = jnp.bfloat16
CORES = 2
UNROLL = 64
BIG = 44 << 20
VMEM = pl.BlockSpec(memory_space=pltpu.VMEM)
SMEM = pl.BlockSpec(memory_space=pltpu.SMEM)
HBM = pl.BlockSpec(memory_space=pltpu.HBM)


def call(kernel, args, out_shape, scratch=(), smem=0, hbm=0, limit=8 << 20, flops=0, aliases=None):
    moved = sum(a.size * a.dtype.itemsize for a in (*args, *out_shape))
    return pl.pallas_call(
        kernel,
        out_shape=out_shape,
        in_specs=[SMEM] * smem + [HBM] * hbm + [VMEM] * (len(args) - smem - hbm),
        out_specs=[VMEM] * len(out_shape),
        scratch_shapes=list(scratch),
        input_output_aliases=aliases or {},
        compiler_params=pltpu.CompilerParams(vmem_limit_bytes=limit),
        cost_estimate=pl.CostEstimate(flops=flops, bytes_accessed=moved, transcendentals=0),
    )(*args)


def shape(dims, dtype=BF16):
    return jax.ShapeDtypeStruct(dims, dtype)


def added(*arrays):
    total = arrays[0].astype(F32)
    for a in arrays[1:]:
        total = total + a.astype(F32)
    return total.astype(BF16)


def lanes(which, half):
    return pl.ds(pl.multiple_of(which * half, half), half)


def place(major, minor, core, block):
    return ((major * 4 + minor) * CORES + core) * 2 + block


PLACES = [(j, n, c, b) for j in range(4) for n in range(4) for c in range(CORES) for b in range(2)]


def row_place(coord_ref, at_ref, s):
    r = coord_ref[0, s]
    core, axes = at_ref[1], (at_ref[2], at_ref[3])
    along_x, along_y = jnp.right_shift(r, 4), jnp.bitwise_and(jnp.right_shift(r, 1), 3)
    major = jnp.bitwise_and(jnp.where(core == 0, along_x, along_y) - axes[0], 3)
    minor = jnp.bitwise_and(jnp.where(core == 0, along_y, along_x) - axes[1], 3)
    own = jnp.bitwise_xor(jnp.bitwise_and(jnp.right_shift(r, 3), 1), core)
    return place(major, minor, own, jnp.bitwise_and(r, 1))


def own_kernel(first, out, sem):
    copy = pltpu.make_async_copy(first, out, sem)
    copy.start()
    copy.wait()


def block_copy(blocks_in, blocks, sems, t):
    part = pl.ds(t * UNROLL, UNROLL)
    return pltpu.make_async_copy(blocks_in.at[part], blocks.at[part], sems.at[t])


def forward_kernel(nz, coord_ref, count_ref, at_ref, blocks_in, *refs):
    pieces, (send_a, send_b, keep_a, keep_b, blocks, turned, feat, acc, sems) = refs[:nz], refs[nz:]
    size = blocks.shape[1]
    turns = blocks.shape[0] // UNROLL
    shard = pieces[0].shape[0]
    half = acc.shape[2] // 2
    z, core = at_ref[0], at_ref[1]
    for t in range(turns):
        block_copy(blocks_in, blocks, sems, t).start()
    rows = acc.shape[0] - 1

    def clear(r, carry):
        acc[r] = jnp.zeros(acc.shape[1:], F32)
        return carry

    lax.fori_loop(0, rows, clear, 0)
    for dz in range(nz):
        at = pl.multiple_of(lax.rem(z + dz, nz) * shard, shard)
        turned[pl.ds(at, shard), :] = pieces[dz][...]
    for c in range(feat.shape[0]):
        feat[c] = turned[:, c * size : (c + 1) * size].T
    count = count_ref[0]

    def turn(t, carry):
        block_copy(blocks_in, blocks, sems, t).wait()
        for u in range(UNROLL):
            s = t * UNROLL + u
            r = jnp.where(s < count, row_place(coord_ref, at_ref, s), rows)
            acc[r] += jnp.dot(blocks[s], feat[coord_ref[1, s]], preferred_element_type=F32)
        return carry

    lax.fori_loop(0, turns, turn, 0)
    for major, minor, c, b in PLACES:
        r = place(major, minor, c, b)
        for j, n, k, out_a, out_b, which in (
            (minor, major, 1 - c, send_a, send_b, 1 - core),
            (major, minor, c, keep_a, keep_b, core),
        ):
            value = acc[r, :, lanes(which, half)].astype(BF16)
            to = pl.ds((k * 2 + b) * size, size)
            if j == 2:
                out_a[n, to, :] = value
            else:
                out_b[(1, 3, 0).index(j), n, to, :] = value


def first_sum_kernel(keep_a, recv_a, passed_in, low, high, passed):
    low[...] = added(keep_a[:2], recv_a[:2])
    high[...] = added(keep_a[2:], recv_a[2:])


def second_sum_kernel(keep_b, recv_b, low, high, near_1, near_3):
    near_1[:2] = added(keep_b[0, :2], recv_b[0, :2], low[...])
    near_1[2:] = added(keep_b[0, 2:], recv_b[0, 2:])
    near_3[:2] = added(keep_b[1, :2], recv_b[1, :2])
    near_3[2:] = added(keep_b[1, 2:], recv_b[1, 2:], high[...])


def third_sum_kernel(keep_b, recv_b, minus, plus, *outs):
    for d in range(4):
        outs[d][...] = added(keep_b[2, d], recv_b[2, d], minus[d], plus[d])


def fourth_sum_kernel(a, b, c, d, own, send):
    rows = own.shape[0]
    own[...] = added(*(r[:rows] for r in (a, b, c, d)))
    send[...] = added(*(r[rows:] for r in (a, b, c, d)))


def middle_kernel(at_ref, own, other, weight, cotangent, act, back_own, send, w_keep, agg, back, terms):
    rows, half = own.shape
    core = at_ref[1]
    agg[:, lanes(core, half)] = own[...]
    agg[:, lanes(1 - core, half)] = other[...]
    pre = jnp.dot(agg[...], weight[...], preferred_element_type=F32)
    sigma = jax.nn.sigmoid(pre)
    grad = (cotangent[...].astype(F32) * sigma * (1.0 + pre * (1.0 - sigma))).astype(BF16)
    back[...] = lax.dot_general(
        grad, weight[...], (((1,), (1,)), ((), ())), preferred_element_type=F32
    ).astype(BF16)
    back_own[...] = back[:, lanes(core, half)]
    send[:rows, :] = back[:, lanes(1 - core, half)]
    act[...] = (pre * sigma).astype(BF16)
    terms[...] = lax.dot_general(
        agg[...], grad, (((0,), (0,)), ((), ())), preferred_element_type=F32
    )
    step = half // 4
    for n in range(4):
        own_at = pl.multiple_of(core * half + lax.rem(at_ref[3] + n, 4) * step, step)
        send_at = pl.multiple_of((1 - core) * half + lax.rem(at_ref[2] + n, 4) * step, step)
        for k in range(2):
            columns = slice(k * half, (k + 1) * half)
            to = (n * 2 + k) * step
            w_keep[to : to + step, :] = terms[pl.ds(own_at, step), columns]
            send[rows + to : rows + to + step, :] = terms[pl.ds(send_at, step), columns].astype(BF16)


def in_order(table, first, *pieces):
    n = len(pieces)
    for d, piece in enumerate(pieces):
        table[lax.rem(first + d, n)] = piece.astype(F32)
    total = table[0]
    for d in range(1, n):
        total = total + table[d]
    return total


def pair_kernel(own, recv, w_keep, *outs):
    rows, part = own.shape[0], w_keep.shape[0] // 4
    for d, out in enumerate(outs):
        n = (-d) % 4 * part
        out[:rows, :] = own[...]
        out[rows : 2 * rows, :] = recv[:rows]
        out[2 * rows :, :] = added(w_keep[n : n + part], recv[rows + n : rows + n + part])


def line_kernel(a, b, c, d, out):
    whole = (out.shape[0] - a.shape[0]) // 3
    for k, ref in enumerate((a, b, c, d)):
        out[k * whole : (k + 1) * whole, :] = ref[:whole]
    out[4 * whole :, :] = added(*(ref[whole:] for ref in (a, b, c, d)))


def halves_kernel(minus, plus, passed_in, low, high, between, passed):
    rows = high.shape[0]
    low[:rows, :] = minus[:rows]
    low[rows:, :] = minus[2 * rows :]
    high[...] = plus[rows : 2 * rows]
    between[: 2 * rows, :] = minus[: 2 * rows]
    between[2 * rows :, :] = plus[: 2 * rows]


def ring_kernel(up, up_term, down, down_term, up_out, down_out):
    rows = up_term.shape[0]
    for got, term, out in ((up, up_term, up_out), (down, down_term, down_out)):
        out[:rows, :] = added(got[:rows], term[...])
        out[rows:, :] = got[rows:]


def third_ring_kernel(at_ref, up, up_term, down, own_term, *refs):
    w, opposite, up_1, down_1, up_2, down_2, up_out, own_out, w_out, table = refs
    rows = up_term.shape[0]
    up_out[...] = added(up[:rows], up_term[...])
    own_out[...] = down[:rows].astype(F32) + own_term[...].astype(F32)
    tails = (ref[rows:] for ref in (down_1, down_2, down))
    after = (ref[rows:] for ref in (up, up_2, up_1))
    w_out[...] = in_order(table, at_ref[0], w[...], *tails, opposite[...], *after)


def last_ring_kernel(at_ref, up, own, wa, wb, wc, wd, out, w_out):
    total = added(up[...], own[...])
    width = total.shape[1]
    for c in range(out.shape[1] // width):
        out[:, c * width : (c + 1) * width] = total[c * out.shape[0] : (c + 1) * out.shape[0]]
    part = wa.shape[0]
    for d, piece in enumerate((wa, wb, wc, wd)):
        w_out[pl.ds(pl.multiple_of(lax.rem(at_ref[3] + d, 4) * part, part), part), :] = piece[...]


def weight_kernel(at_ref, mine, theirs, out):
    core, half = at_ref[1], out.shape[0] // 2
    step = half // 4
    for which, piece in ((core, mine), (1 - core, theirs)):
        for n in range(4):
            at = pl.ds(pl.multiple_of(which * half + n * step, step), step)
            for k in range(2):
                out[at, k * half : (k + 1) * half] = piece[(n * 2 + k) * step : (n * 2 + k + 1) * step]


def backward_kernel(nz, coord_ref, count_ref, at_ref, blocks_in, *refs):
    mine, (line, between, low, high), (w, *outs) = refs[:5], refs[5:9], refs[9 : 10 + nz]
    blocks, back, acc, turned, table, sems = refs[10 + nz :]
    rows = between.shape[0] // 2
    theirs = (line, between.at[:rows], between.at[rows:], low, high)
    size = blocks.shape[1]
    turns = blocks.shape[0] // UNROLL
    half = back.shape[2] // 2
    z, core = at_ref[0], at_ref[1]
    for t in range(turns):
        block_copy(blocks_in, blocks, sems, t).start()
    for (own, minus, plus, low, high), is_mine in ((mine, True), (theirs, False)):
        for major, minor, c, b in PLACES:
            source = {0: own, 3: minus, 1: plus, 2: low if minor < 2 else high}[major]
            k = minor % 2 if major == 2 else minor
            k = ((k * CORES + c) * 2 + b) * size
            r = place(major, minor, c, b) if is_mine else place(minor, major, 1 - c, b)
            to = lanes(core if is_mine else 1 - core, half)
            back[r, :, to] = source[k : k + size, :]
    cols = acc.shape[0] - 1
    for c in range(cols):
        acc[c] = jnp.zeros(acc.shape[1:], F32)
    count = count_ref[0]

    def turn(t, carry):
        block_copy(blocks_in, blocks, sems, t).wait()
        for u in range(UNROLL):
            s = t * UNROLL + u
            c = jnp.where(s < count, coord_ref[1, s], cols)
            acc[c] += lax.dot_general(
                blocks[s], back[row_place(coord_ref, at_ref, s)], (((0,), (0,)), ((), ())), preferred_element_type=F32
            )
        return carry

    lax.fori_loop(0, turns, turn, 0)
    own, minus, plus, low, high = mine
    rows = w.shape[0]
    tails = (ref[ref.shape[0] - rows :] for ref in (own, plus, low, minus))
    w[...] = in_order(table, at_ref[2], *tails).astype(BF16)
    for out in (outs[4], outs[5]):
        out[out.shape[0] - rows :, :] = w[...]
    shard = turned.shape[1] // nz
    for c in range(cols):
        turned[c] = acc[c].astype(BF16).T
        for dz in range(nz):
            at = pl.multiple_of(lax.rem(z + dz, nz) * shard, shard)
            outs[dz][c * shard : (c + 1) * shard, :] = turned[c, pl.ds(at, shard), :]


def local(features, weight, cotangent, block_values, block_coords, block_counts):
    blocks, coords = block_values[0, 0], block_coords[0, 0]
    nz, ny = lax.axis_size("row"), lax.axis_size("rep")
    ncol = lax.axis_size("col")
    nx = ncol // CORES
    z, y = lax.axis_index("row"), lax.axis_index("rep")
    x, core = lax.axis_index("col") // CORES, lax.axis_index("col") % CORES
    at = jnp.stack([z, core, jnp.where(core == 0, x, y), jnp.where(core == 0, y, x)]).astype(jnp.int32)
    count = block_counts[0]
    coords = coords.T
    slots, size, _ = blocks.shape
    rows_dev, width = cotangent.shape
    half = width // 2
    nodes, shard = features.shape
    flops = 2 * slots * size * size * width
    turns = slots // UNROLL

    def move(a, axis, d):
        pairs = []
        for i in range(nx):
            for c in range(CORES):
                for j in range(ny):
                    along_x = (axis == "major") == (c == 0)
                    to = ((i + d) % nx, j) if along_x else (i, (j + d) % ny)
                    pairs.append(((i * CORES + c) * ny + j, (to[0] * CORES + c) * ny + to[1]))
        return lax.ppermute(a, ("col", "rep"), pairs)

    def swap(a):
        return lax.ppermute(a, "col", [(i, i ^ 1) for i in range(ncol)])

    def along_z(a, d):
        return lax.ppermute(a, "row", [(i, (i + d) % nz) for i in range(nz)])

    def flip_z(a, bit):
        return lax.ppermute(a, "row", [(i, i ^ bit) for i in range(nz)])

    shards = [None] * nz
    shards[0] = features.T
    for k in range(1, nz // 2 + 1):
        shards[nz - k] = along_z(shards[(nz - k + 1) % nz], 1)
        if k < nz // 2:
            shards[k] = along_z(shards[k - 1], -1)

    (shards[0],) = call(
        own_kernel, (shards[0],), [shape((shard, nodes))], [pltpu.SemaphoreType.DMA], hbm=1
    )
    pair = CORES * rows_dev
    part_a, part_b = shape((4, pair, half)), shape((3, 4, pair, half))
    row_blocks = len(PLACES)
    send_a, send_b, keep_a, keep_b = call(
        functools.partial(forward_kernel, nz),
        (coords, count, at, blocks, *shards),
        [part_a, part_b, part_a, part_b],
        [
            pltpu.VMEM(blocks.shape, BF16),
            pltpu.VMEM((width, nodes), BF16),
            pltpu.VMEM((nodes // size, size, width), BF16),
            pltpu.VMEM((row_blocks + 1, size, width), F32),
            pltpu.SemaphoreType.DMA((turns,)),
        ],
        smem=3,
        hbm=1,
        limit=BIG,
        flops=flops,
    )

    recv_a = swap(send_a)
    two, four, one = shape((2, pair, half)), shape((4, pair, half)), shape((pair, half))
    low, high, send_b = call(first_sum_kernel, (keep_a, recv_a, send_b), [two, two, part_b], aliases={2: 2})
    low, high, recv_b = move(low, "major", 1), move(high, "major", -1), swap(send_b)
    near_1, near_3 = call(second_sum_kernel, (keep_b, recv_b, low, high), [four] * 2)
    minus, plus = move(near_1, "major", 1), move(near_3, "major", -1)
    sums = call(third_sum_kernel, (keep_b, recv_b, minus, plus), [one] * 4)
    sums = [sums[0]] + [move(sums[d], "minor", d) for d in (1, 2, 3)]
    mine = shape((rows_dev, half))
    agg_own, agg_send = call(fourth_sum_kernel, sums, [mine] * 2)

    part = width // 4
    activations, back_own, send, w_keep = call(
        middle_kernel,
        (at, agg_own, swap(agg_send), weight, cotangent),
        [shape((rows_dev, width)), mine, shape((rows_dev + width, half)), shape((width, half), F32)],
        [pltpu.VMEM((rows_dev, width), BF16)] * 2 + [pltpu.VMEM((width, width), F32)],
        smem=1,
    )

    near = call(pair_kernel, (back_own, swap(send), w_keep), [shape((pair + part, half))] * 4)
    near = [near[0]] + [move(near[d], "minor", -d) for d in (1, 2, 3)]
    (line,) = call(line_kernel, near, [shape((4 * pair + part, half))])
    minus, plus = move(line, "major", 1), move(line, "major", -1)
    sibling_line = swap(line)
    low, high, between, sibling_line = call(
        halves_kernel,
        (minus, plus, sibling_line),
        [
            shape((2 * pair + part, half)),
            shape((2 * pair, half)),
            shape((8 * pair, half)),
            shape(line.shape),
        ],
        aliases={2: 3},
    )
    low, high, between = move(low, "major", 1), move(high, "major", -1), swap(between)
    rows_all = (line, minus, plus, low, high, sibling_line, between, swap(low), swap(high))

    cells = shard * nodes // size
    ring, ring_w = shape((cells, size)), shape((cells + part, size))
    w, *terms = call(
        functools.partial(backward_kernel, nz),
        (coords, count, at, blocks, *rows_all),
        [shape((part, half))] + [ring_w if k in (4, 5) else ring for k in range(nz)],
        [
            pltpu.VMEM(blocks.shape, BF16),
            pltpu.VMEM((row_blocks, size, width), BF16),
            pltpu.VMEM((nodes // size + 1, size, width), F32),
            pltpu.VMEM((nodes // size, width, size), BF16),
            pltpu.VMEM((4, part, half), F32),
            pltpu.SemaphoreType.DMA((turns,)),
        ],
        smem=3,
        hbm=1,
        limit=BIG,
        flops=flops,
    )
    up_1, down_1 = along_z(terms[4], 1), along_z(terms[5], -1)
    up, down = call(ring_kernel, (up_1, terms[3], down_1, terms[6]), [ring_w] * 2)
    up_2, down_2 = along_z(up, 1), along_z(down, -1)
    up, down = call(ring_kernel, (up_2, terms[2], down_2, terms[7]), [ring_w] * 2)
    up_3, down_3 = along_z(up, 1), along_z(down, -1)
    up, own, w = call(
        third_ring_kernel,
        (at, up_3, terms[1], down_3, terms[0], w, flip_z(w, 4), up_1, down_1, up_2, down_2),
        [ring, shape((cells, size), F32), shape((part, half), F32)],
        [pltpu.VMEM((nz, part, half), F32)],
        smem=1,
    )
    w = [w] + [move(w, "minor", -d) for d in (1, 2, 3)]
    input_grad, w = call(
        last_ring_kernel,
        (at, along_z(up, 1), own, *w),
        [shape((shard, nodes)), shape((width, half), F32)],
        smem=1,
    )
    (weight_grad,) = call(weight_kernel, (at, w, swap(w)), [shape((width, width), F32)], smem=1)
    return activations, input_grad.T, weight_grad


def solution(mesh):
    in_specs = (
        P(("col", "rep"), "row"),
        P(),
        P(("row", "col", "rep"), None),
        P("row", ("col", "rep"), None, None, None),
        P("row", ("col", "rep"), None, None),
        P("row", ("col", "rep")),
    )
    out_specs = (P(("row", "col", "rep"), None), P(("col", "rep"), "row"), P())
    return jax.shard_map(local, mesh=mesh, in_specs=in_specs, out_specs=out_specs, check_vma=False)
```

```python
import functools

import jax
import jax.numpy as jnp
from jax import lax
from jax.experimental import pallas as pl
from jax.experimental.pallas import tpu as pltpu
from jax.sharding import PartitionSpec as P

F32 = jnp.float32
BF16 = jnp.bfloat16
CORES = 2
UNROLL = 64
BIG = 44 << 20
VMEM = pl.BlockSpec(memory_space=pltpu.VMEM)
SMEM = pl.BlockSpec(memory_space=pltpu.SMEM)
HBM = pl.BlockSpec(memory_space=pltpu.HBM)


def call(kernel, args, out_shape, scratch=(), smem=0, hbm=0, limit=8 << 20, flops=0, aliases=None):
    moved = sum(a.size * a.dtype.itemsize for a in (*args, *out_shape))
    return pl.pallas_call(
        kernel,
        out_shape=out_shape,
        in_specs=[SMEM] * smem + [HBM] * hbm + [VMEM] * (len(args) - smem - hbm),
        out_specs=[VMEM] * len(out_shape),
        scratch_shapes=list(scratch),
        input_output_aliases=aliases or {},
        compiler_params=pltpu.CompilerParams(vmem_limit_bytes=limit),
        cost_estimate=pl.CostEstimate(flops=flops, bytes_accessed=moved, transcendentals=0),
    )(*args)


def shape(dims, dtype=BF16):
    return jax.ShapeDtypeStruct(dims, dtype)


def added(*arrays):
    total = arrays[0].astype(F32)
    for a in arrays[1:]:
        total = total + a.astype(F32)
    return total.astype(BF16)


def lanes(which, half):
    return pl.ds(pl.multiple_of(which * half, half), half)


def place(major, minor, core, block):
    return ((major * 4 + minor) * CORES + core) * 2 + block


PLACES = [(j, n, c, b) for j in range(4) for n in range(4) for c in range(CORES) for b in range(2)]


def row_place(coord_ref, at_ref, s):
    r = coord_ref[0, s]
    core, axes = at_ref[1], (at_ref[2], at_ref[3])
    along_x, along_y = jnp.right_shift(r, 4), jnp.bitwise_and(jnp.right_shift(r, 1), 3)
    major = jnp.bitwise_and(jnp.where(core == 0, along_x, along_y) - axes[0], 3)
    minor = jnp.bitwise_and(jnp.where(core == 0, along_y, along_x) - axes[1], 3)
    own = jnp.bitwise_xor(jnp.bitwise_and(jnp.right_shift(r, 3), 1), core)
    return place(major, minor, own, jnp.bitwise_and(r, 1))


def own_kernel(first, out, sem):
    copy = pltpu.make_async_copy(first, out, sem)
    copy.start()
    copy.wait()


FIRST = ((2, 0), (2, 1), (2, 2), (2, 3), (1, 2), (1, 3), (3, 0), (3, 1))
SECOND = ((0, 0), (0, 1), (0, 2), (0, 3), (1, 0), (1, 1), (3, 2), (3, 3))


def block_copy(blocks_in, blocks, sems, t):
    part = pl.ds(t * UNROLL, UNROLL)
    return pltpu.make_async_copy(blocks_in.at[part], blocks.at[part], sems.at[t])


def forward_kernel(nz, coord_ref, count_ref, at_ref, blocks_in, *refs):
    pieces, (send_a, send_b, keep_a, keep_b, blocks, turned, feat, acc, sems) = refs[:nz], refs[nz:]
    size = blocks.shape[1]
    turns = blocks.shape[0] // UNROLL
    shard = pieces[0].shape[0]
    half = acc.shape[2] // 2
    z, core = at_ref[0], at_ref[1]
    for t in range(turns):
        block_copy(blocks_in, blocks, sems, t).start()
    rows = acc.shape[0] - 1

    def clear(r, carry):
        acc[r] = jnp.zeros(acc.shape[1:], F32)
        return carry

    lax.fori_loop(0, rows, clear, 0)
    for dz in range(nz):
        at = pl.multiple_of(lax.rem(z + dz, nz) * shard, shard)
        turned[pl.ds(at, shard), :] = pieces[dz][...]
    for c in range(feat.shape[0]):
        feat[c] = turned[:, c * size : (c + 1) * size].T
    count = count_ref[0]

    def turn(t, carry):
        block_copy(blocks_in, blocks, sems, t).wait()
        for u in range(UNROLL):
            s = t * UNROLL + u
            r = jnp.where(s < count, row_place(coord_ref, at_ref, s), rows)
            acc[r] += jnp.dot(blocks[s], feat[coord_ref[1, s]], preferred_element_type=F32)
        return carry

    lax.fori_loop(0, turns, turn, 0)
    for major, minor, c, b in PLACES:
        r = place(major, minor, c, b)
        for j, n, k, out_a, out_b, which in (
            (minor, major, 1 - c, send_a, send_b, 1 - core),
            (major, minor, c, keep_a, keep_b, core),
        ):
            value = acc[r, :, lanes(which, half)].astype(BF16)
            to = pl.ds((k * 2 + b) * size, size)
            out = out_a if (j, n) in FIRST else out_b
            out[(FIRST if (j, n) in FIRST else SECOND).index((j, n)), to, :] = value


def first_sum_kernel(keep_a, recv_a, passed_in, low, high, free_1, free_3, passed):
    for k, out in enumerate((low, high, free_1, free_3)):
        out[...] = added(keep_a[2 * k : 2 * k + 2], recv_a[2 * k : 2 * k + 2])


def second_sum_kernel(keep_b, recv_b, low, high, near_1, near_3):
    near_1[...] = added(keep_b[4:6], recv_b[4:6], low[...])
    near_3[...] = added(keep_b[6:], recv_b[6:], high[...])


def third_sum_kernel(keep_b, recv_b, free_1, free_3, near_1, near_3, *outs):
    for d in range(4):
        minus, plus = (near_1, free_3) if d < 2 else (free_1, near_3)
        outs[d][...] = added(keep_b[d], recv_b[d], minus[d % 2], plus[d % 2])


def fourth_sum_kernel(a, b, c, d, own, send):
    rows = own.shape[0]
    own[...] = added(*(r[:rows] for r in (a, b, c, d)))
    send[...] = added(*(r[rows:] for r in (a, b, c, d)))


def middle_kernel(at_ref, own, other, weight, cotangent, act, back_own, send, w_keep, agg, back, terms):
    rows, half = own.shape
    core = at_ref[1]
    agg[:, lanes(core, half)] = own[...]
    agg[:, lanes(1 - core, half)] = other[...]
    pre = jnp.dot(agg[...], weight[...], preferred_element_type=F32)
    sigma = jax.nn.sigmoid(pre)
    grad = (cotangent[...].astype(F32) * sigma * (1.0 + pre * (1.0 - sigma))).astype(BF16)
    back[...] = lax.dot_general(
        grad, weight[...], (((1,), (1,)), ((), ())), preferred_element_type=F32
    ).astype(BF16)
    back_own[...] = back[:, lanes(core, half)]
    send[:rows, :] = back[:, lanes(1 - core, half)]
    act[...] = (pre * sigma).astype(BF16)
    terms[...] = lax.dot_general(
        agg[...], grad, (((0,), (0,)), ((), ())), preferred_element_type=F32
    )
    step = half // 4
    for n in range(4):
        own_at = pl.multiple_of(core * half + lax.rem(at_ref[3] + n, 4) * step, step)
        send_at = pl.multiple_of((1 - core) * half + lax.rem(at_ref[2] + n, 4) * step, step)
        for k in range(2):
            columns = slice(k * half, (k + 1) * half)
            to = (n * 2 + k) * step
            w_keep[to : to + step, :] = terms[pl.ds(own_at, step), columns]
            send[rows + to : rows + to + step, :] = terms[pl.ds(send_at, step), columns].astype(BF16)


def in_order(table, first, *pieces):
    n = len(pieces)
    for d, piece in enumerate(pieces):
        table[lax.rem(first + d, n)] = piece.astype(F32)
    total = table[0]
    for d in range(1, n):
        total = total + table[d]
    return total


def pair_kernel(own, recv, w_keep, *outs):
    rows, part = own.shape[0], w_keep.shape[0] // 4
    for d, out in enumerate(outs):
        n = (-d) % 4 * part
        out[:rows, :] = own[...]
        out[rows : 2 * rows, :] = recv[:rows]
        out[2 * rows :, :] = added(w_keep[n : n + part], recv[rows + n : rows + n + part])


def line_kernel(a, b, c, d, head, foot, whole):
    rows = whole.shape[0] // 4
    for k, ref in enumerate((a, b, c, d)):
        whole[k * rows : (k + 1) * rows, :] = ref[:rows]
        part = head if k < 2 else foot
        part[k % 2 * rows : (k % 2 + 1) * rows, :] = ref[:rows]
    head[2 * rows :, :] = added(*(ref[rows:] for ref in (a, b, c, d)))


def ring_kernel(up, up_term, down, down_term, up_out, down_out):
    rows = up_term.shape[0]
    for got, term, out in ((up, up_term, up_out), (down, down_term, down_out)):
        out[:rows, :] = added(got[:rows], term[...])
        out[rows:, :] = got[rows:]


def third_ring_kernel(up, up_term, down, own_term, up_out, own_out):
    rows = up_term.shape[0]
    up_out[:rows, :] = added(up[:rows], up_term[...])
    up_out[rows:, :] = up[rows:]
    own_out[...] = down[:rows].astype(F32) + own_term[...].astype(F32)


def last_ring_kernel(at_ref, up, own, w, up_1, up_2, up_3, down_1, down_2, down_3, w_out, out, table):
    rows = own.shape[0]
    tails = (ref[rows:] for ref in (down_1, down_2, down_3, up, up_3, up_2, up_1))
    w_out[...] = in_order(table, at_ref[0], w[...], *tails)
    total = added(up[:rows], own[...])
    width = total.shape[1]
    for c in range(out.shape[1] // width):
        out[:, c * width : (c + 1) * width] = total[c * out.shape[0] : (c + 1) * out.shape[0]]


def gather_kernel(at_ref, wa, wb, wc, wd, out):
    part = wa.shape[0]
    for d, piece in enumerate((wa, wb, wc, wd)):
        out[pl.ds(pl.multiple_of(lax.rem(at_ref[3] + d, 4) * part, part), part), :] = piece[...]


def weight_kernel(at_ref, mine, theirs, out):
    core, half = at_ref[1], out.shape[0] // 2
    step = half // 4
    for which, piece in ((core, mine), (1 - core, theirs)):
        for n in range(4):
            at = pl.ds(pl.multiple_of(which * half + n * step, step), step)
            for k in range(2):
                out[at, k * half : (k + 1) * half] = piece[(n * 2 + k) * step : (n * 2 + k + 1) * step]


def backward_kernel(nz, coord_ref, count_ref, at_ref, blocks_in, *refs):
    head, foot, minus_head, minus_foot, plus_head, plus_foot, low, high = refs[:8]
    line, *swapped = refs[8:15]
    w, *outs = refs[15 : 16 + nz]
    blocks, back, acc, turned, table, sems = refs[16 + nz :]
    quarter = foot.shape[0]
    mine = ((head, foot), (plus_head, plus_foot), (low, high), (minus_head, minus_foot))
    theirs = ((line.at[:quarter], line.at[quarter:]), swapped[2:4], swapped[4:], swapped[:2])
    size = blocks.shape[1]
    turns = blocks.shape[0] // UNROLL
    half = back.shape[2] // 2
    z, core = at_ref[0], at_ref[1]
    for t in range(turns):
        block_copy(blocks_in, blocks, sems, t).start()
    for sources, is_mine in ((mine, True), (theirs, False)):
        for major, minor, c, b in PLACES:
            source = sources[major][minor // 2]
            k = ((minor % 2 * CORES + c) * 2 + b) * size
            r = place(major, minor, c, b) if is_mine else place(minor, major, 1 - c, b)
            to = lanes(core if is_mine else 1 - core, half)
            back[r, :, to] = source[k : k + size, :]
    cols = acc.shape[0] - 1
    for c in range(cols):
        acc[c] = jnp.zeros(acc.shape[1:], F32)
    count = count_ref[0]

    def turn(t, carry):
        block_copy(blocks_in, blocks, sems, t).wait()
        for u in range(UNROLL):
            s = t * UNROLL + u
            c = jnp.where(s < count, coord_ref[1, s], cols)
            acc[c] += lax.dot_general(
                blocks[s], back[row_place(coord_ref, at_ref, s)], (((0,), (0,)), ((), ())), preferred_element_type=F32
            )
        return carry

    lax.fori_loop(0, turns, turn, 0)
    rows = w.shape[0]
    tails = (ref[quarter:] for ref in (head, plus_head, low, minus_head))
    w[...] = in_order(table, at_ref[2], *tails).astype(BF16)
    for out in (outs[4], outs[5]):
        out[out.shape[0] - rows :, :] = w[...]
    shard = turned.shape[1] // nz
    for c in range(cols):
        turned[c] = acc[c].astype(BF16).T
        for dz in range(nz):
            at = pl.multiple_of(lax.rem(z + dz, nz) * shard, shard)
            outs[dz][c * shard : (c + 1) * shard, :] = turned[c, pl.ds(at, shard), :]


def local(features, weight, cotangent, block_values, block_coords, block_counts):
    blocks, coords = block_values[0, 0], block_coords[0, 0]
    nz, ny = lax.axis_size("row"), lax.axis_size("rep")
    ncol = lax.axis_size("col")
    nx = ncol // CORES
    z, y = lax.axis_index("row"), lax.axis_index("rep")
    x, core = lax.axis_index("col") // CORES, lax.axis_index("col") % CORES
    at = jnp.stack([z, core, jnp.where(core == 0, x, y), jnp.where(core == 0, y, x)]).astype(jnp.int32)
    count = block_counts[0]
    coords = coords.T
    slots, size, _ = blocks.shape
    rows_dev, width = cotangent.shape
    half = width // 2
    nodes, shard = features.shape
    flops = 2 * slots * size * size * width
    turns = slots // UNROLL

    def move(a, axis, d):
        pairs = []
        for i in range(nx):
            for c in range(CORES):
                for j in range(ny):
                    along_x = (axis == "major") == (c == 0)
                    to = ((i + d) % nx, j) if along_x else (i, (j + d) % ny)
                    pairs.append(((i * CORES + c) * ny + j, (to[0] * CORES + c) * ny + to[1]))
        return lax.ppermute(a, ("col", "rep"), pairs)

    def swap(a):
        return lax.ppermute(a, "col", [(i, i ^ 1) for i in range(ncol)])

    def along_z(a, d):
        return lax.ppermute(a, "row", [(i, (i + d) % nz) for i in range(nz)])

    shards = [None] * nz
    shards[0] = features.T
    for k in range(1, nz // 2 + 1):
        shards[nz - k] = along_z(shards[(nz - k + 1) % nz], 1)
        if k < nz // 2:
            shards[k] = along_z(shards[k - 1], -1)

    (shards[0],) = call(
        own_kernel, (shards[0],), [shape((shard, nodes))], [pltpu.SemaphoreType.DMA], hbm=1
    )
    pair = CORES * rows_dev
    part_a = part_b = shape((8, pair, half))
    row_blocks = len(PLACES)
    send_a, send_b, keep_a, keep_b = call(
        functools.partial(forward_kernel, nz),
        (coords, count, at, blocks, *shards),
        [part_a, part_b, part_a, part_b],
        [
            pltpu.VMEM(blocks.shape, BF16),
            pltpu.VMEM((width, nodes), BF16),
            pltpu.VMEM((nodes // size, size, width), BF16),
            pltpu.VMEM((row_blocks + 1, size, width), F32),
            pltpu.SemaphoreType.DMA((turns,)),
        ],
        smem=3,
        hbm=1,
        limit=BIG,
        flops=flops,
    )

    recv_a = swap(send_a)
    two, one = shape((2, pair, half)), shape((pair, half))
    low, high, free_1, free_3, send_b = call(
        first_sum_kernel, (keep_a, recv_a, send_b), [two] * 4 + [part_b], aliases={2: 4}
    )
    low, high, recv_b = move(low, "major", 1), move(high, "major", -1), swap(send_b)
    free_1, free_3 = move(free_1, "major", 1), move(free_3, "major", -1)
    near_1, near_3 = call(second_sum_kernel, (keep_b, recv_b, low, high), [two] * 2)
    arrived = (free_1, free_3, move(near_1, "major", 1), move(near_3, "major", -1))
    sums = call(third_sum_kernel, (keep_b, recv_b, *arrived), [one] * 4)
    sums = [sums[0]] + [move(sums[d], "minor", d) for d in (1, 2, 3)]
    mine = shape((rows_dev, half))
    agg_own, agg_send = call(fourth_sum_kernel, sums, [mine] * 2)

    part = width // 4
    activations, back_own, send, w_keep = call(
        middle_kernel,
        (at, agg_own, swap(agg_send), weight, cotangent),
        [shape((rows_dev, width)), mine, shape((rows_dev + width, half)), shape((width, half), F32)],
        [pltpu.VMEM((rows_dev, width), BF16)] * 2 + [pltpu.VMEM((width, width), F32)],
        smem=1,
    )

    near = call(pair_kernel, (back_own, swap(send), w_keep), [shape((pair + part, half))] * 4)
    near = [near[0]] + [move(near[d], "minor", -d) for d in (1, 2, 3)]
    head, foot, line = call(
        line_kernel, near, [shape((2 * pair + part, half)), shape((2 * pair, half)), shape((4 * pair, half))]
    )
    minus_head, plus_foot = move(head, "major", 1), move(foot, "major", -1)
    minus_foot, plus_head = move(foot, "major", 1), move(head, "major", -1)
    low, high = move(minus_head, "major", 1), move(plus_foot, "major", -1)
    far = (minus_head, minus_foot, plus_head, plus_foot, low, high)
    rows_all = (head, foot, *far, swap(line), *(swap(a) for a in far))

    cells = shard * nodes // size
    ring, ring_w = shape((cells, size)), shape((cells + part, size))
    w, *terms = call(
        functools.partial(backward_kernel, nz),
        (coords, count, at, blocks, *rows_all),
        [shape((part, half))] + [ring_w if k in (4, 5) else ring for k in range(nz)],
        [
            pltpu.VMEM(blocks.shape, BF16),
            pltpu.VMEM((row_blocks, size, width), BF16),
            pltpu.VMEM((nodes // size + 1, size, width), F32),
            pltpu.VMEM((nodes // size, width, size), BF16),
            pltpu.VMEM((4, part, half), F32),
            pltpu.SemaphoreType.DMA((turns,)),
        ],
        smem=3,
        hbm=1,
        limit=BIG,
        flops=flops,
    )
    up_1, down_1 = along_z(terms[4], 1), along_z(terms[5], -1)
    up, down = call(ring_kernel, (up_1, terms[3], down_1, terms[6]), [ring_w] * 2)
    up_2, down_2 = along_z(up, 1), along_z(down, -1)
    up, down = call(ring_kernel, (up_2, terms[2], down_2, terms[7]), [ring_w] * 2)
    up_3, down_3 = along_z(up, 1), along_z(down, -1)
    up, own = call(
        third_ring_kernel,
        (up_3, terms[1], down_3, terms[0]),
        [ring_w, shape((cells, size), F32)],
    )
    w, input_grad = call(
        last_ring_kernel,
        (at, along_z(up, 1), own, w, up_1, up_2, up_3, down_1, down_2, down_3),
        [shape((part, half), F32), shape((shard, nodes))],
        [pltpu.VMEM((nz, part, half), F32)],
        smem=1,
    )
    w = [w] + [move(w, "minor", -d) for d in (1, 2, 3)]
    (w,) = call(gather_kernel, (at, *w), [shape((width, half), F32)], smem=1)
    (weight_grad,) = call(weight_kernel, (at, w, swap(w)), [shape((width, width), F32)], smem=1)
    return activations, input_grad.T, weight_grad


def solution(mesh):
    in_specs = (
        P(("col", "rep"), "row"),
        P(),
        P(("row", "col", "rep"), None),
        P("row", ("col", "rep"), None, None, None),
        P("row", ("col", "rep"), None, None),
        P("row", ("col", "rep")),
    )
    out_specs = (P(("row", "col", "rep"), None), P(("col", "rep"), "row"), P())
    return jax.shard_map(local, mesh=mesh, in_specs=in_specs, out_specs=out_specs, check_vma=False)
```

```python
import functools

import jax
import jax.numpy as jnp
from jax import lax
from jax.experimental import pallas as pl
from jax.experimental.pallas import tpu as pltpu
from jax.sharding import PartitionSpec as P

F32 = jnp.float32
BF16 = jnp.bfloat16
CORES = 2
UNROLL = 32
BIG = 44 << 20
VMEM = pl.BlockSpec(memory_space=pltpu.VMEM)
SMEM = pl.BlockSpec(memory_space=pltpu.SMEM)
HBM = pl.BlockSpec(memory_space=pltpu.HBM)


def call(kernel, args, out_shape, scratch=(), smem=0, hbm=0, limit=8 << 20, flops=0, aliases=None):
    moved = sum(a.size * a.dtype.itemsize for a in (*args, *out_shape))
    return pl.pallas_call(
        kernel,
        out_shape=out_shape,
        in_specs=[SMEM] * smem + [HBM] * hbm + [VMEM] * (len(args) - smem - hbm),
        out_specs=[VMEM] * len(out_shape),
        scratch_shapes=list(scratch),
        input_output_aliases=aliases or {},
        compiler_params=pltpu.CompilerParams(vmem_limit_bytes=limit),
        cost_estimate=pl.CostEstimate(flops=flops, bytes_accessed=moved, transcendentals=0),
    )(*args)


def shape(dims, dtype=BF16):
    return jax.ShapeDtypeStruct(dims, dtype)


def added(*arrays):
    total = arrays[0].astype(F32)
    for a in arrays[1:]:
        total = total + a.astype(F32)
    return total.astype(BF16)


def lanes(which, half):
    return pl.ds(pl.multiple_of(which * half, half), half)


def place(major, minor, core, block):
    return ((major * 4 + minor) * CORES + core) * 2 + block


PLACES = [(j, n, c, b) for j in range(4) for n in range(4) for c in range(CORES) for b in range(2)]


def row_place(coord_ref, at_ref, s):
    r = coord_ref[0, s]
    core, axes = at_ref[1], (at_ref[2], at_ref[3])
    along_x, along_y = jnp.right_shift(r, 4), jnp.bitwise_and(jnp.right_shift(r, 1), 3)
    major = jnp.bitwise_and(jnp.where(core == 0, along_x, along_y) - axes[0], 3)
    minor = jnp.bitwise_and(jnp.where(core == 0, along_y, along_x) - axes[1], 3)
    own = jnp.bitwise_xor(jnp.bitwise_and(jnp.right_shift(r, 3), 1), core)
    return place(major, minor, own, jnp.bitwise_and(r, 1))


def own_kernel(first, out, sem):
    copy = pltpu.make_async_copy(first, out, sem)
    copy.start()
    copy.wait()


FIRST = ((2, 0), (2, 1), (2, 2), (2, 3), (1, 2), (1, 3), (3, 0), (3, 1))
SECOND = ((0, 0), (0, 1), (0, 2), (0, 3), (1, 0), (1, 1), (3, 2), (3, 3))


def block_copy(blocks_in, blocks, sems, t):
    part = pl.ds(t * UNROLL, UNROLL)
    return pltpu.make_async_copy(blocks_in.at[part], blocks.at[part], sems.at[t])


def forward_kernel(nz, coord_ref, count_ref, at_ref, blocks_in, *refs):
    pieces, (send_a, send_b, keep_a, keep_b, blocks, turned, feat, acc, sems) = refs[:nz], refs[nz:]
    size = blocks.shape[1]
    turns = blocks.shape[0] // UNROLL
    shard = pieces[0].shape[0]
    half = acc.shape[2] // 2
    z, core = at_ref[0], at_ref[1]
    for t in range(turns):
        block_copy(blocks_in, blocks, sems, t).start()
    rows = acc.shape[0] - 1

    def clear(r, carry):
        acc[r] = jnp.zeros(acc.shape[1:], F32)
        return carry

    lax.fori_loop(0, rows, clear, 0)
    for dz in range(nz):
        at = pl.multiple_of(lax.rem(z + dz, nz) * shard, shard)
        turned[pl.ds(at, shard), :] = pieces[dz][...]
    for c in range(feat.shape[0]):
        feat[c] = turned[:, c * size : (c + 1) * size].T
    count = count_ref[0]

    def turn(t, carry):
        block_copy(blocks_in, blocks, sems, t).wait()
        for u in range(UNROLL):
            s = t * UNROLL + u
            r = jnp.where(s < count, row_place(coord_ref, at_ref, s), rows)
            acc[r] += jnp.dot(blocks[s], feat[coord_ref[1, s]], preferred_element_type=F32)
        return carry

    lax.fori_loop(0, turns, turn, 0)
    for major in range(4):
        for minor in range(4):

            def write(q, carry, major=major, minor=minor):
                r = place(major, minor, 0, 0) + q
                for j, n, k, out_a, out_b, which in (
                    (minor, major, jnp.bitwise_xor(q, 2), send_a, send_b, 1 - core),
                    (major, minor, q, keep_a, keep_b, core),
                ):
                    value = acc[r, :, lanes(which, half)].astype(BF16)
                    out, units = (out_a, FIRST) if (j, n) in FIRST else (out_b, SECOND)
                    out[units.index((j, n)), pl.ds(pl.multiple_of(k * size, size), size), :] = value
                return carry

            lax.fori_loop(0, 4, write, 0)


def first_sum_kernel(keep_a, recv_a, passed_in, low, high, free_1, free_3, passed):
    for k, out in enumerate((low, high, free_1, free_3)):
        out[...] = added(keep_a[2 * k : 2 * k + 2], recv_a[2 * k : 2 * k + 2])


def second_sum_kernel(keep_b, recv_b, low, high, near_1, near_3):
    near_1[...] = added(keep_b[4:6], recv_b[4:6], low[...])
    near_3[...] = added(keep_b[6:], recv_b[6:], high[...])


def third_sum_kernel(keep_b, recv_b, free_1, free_3, near_1, near_3, *outs):
    for d in range(4):
        minus, plus = (near_1, free_3) if d < 2 else (free_1, near_3)
        outs[d][...] = added(keep_b[d], recv_b[d], minus[d % 2], plus[d % 2])


def fourth_sum_kernel(a, b, c, d, own, send):
    rows = own.shape[0]
    own[...] = added(*(r[:rows] for r in (a, b, c, d)))
    send[...] = added(*(r[rows:] for r in (a, b, c, d)))


def middle_kernel(at_ref, own, other, weight, cotangent, act, back_own, send, w_keep, agg, back, terms):
    rows, half = own.shape
    core = at_ref[1]
    agg[:, lanes(core, half)] = own[...]
    agg[:, lanes(1 - core, half)] = other[...]
    pre = jnp.dot(agg[...], weight[...], preferred_element_type=F32)
    sigma = jax.nn.sigmoid(pre)
    grad = (cotangent[...].astype(F32) * sigma * (1.0 + pre * (1.0 - sigma))).astype(BF16)
    back[...] = lax.dot_general(
        grad, weight[...], (((1,), (1,)), ((), ())), preferred_element_type=F32
    ).astype(BF16)
    back_own[...] = back[:, lanes(core, half)]
    send[:rows, :] = back[:, lanes(1 - core, half)]
    act[...] = (pre * sigma).astype(BF16)
    terms[...] = lax.dot_general(
        agg[...], grad, (((0,), (0,)), ((), ())), preferred_element_type=F32
    )
    step = half // 4
    for n in range(4):
        own_at = pl.multiple_of(core * half + lax.rem(at_ref[3] + n, 4) * step, step)
        send_at = pl.multiple_of((1 - core) * half + lax.rem(at_ref[2] + n, 4) * step, step)
        for k in range(2):
            columns = slice(k * half, (k + 1) * half)
            to = (n * 2 + k) * step
            w_keep[to : to + step, :] = terms[pl.ds(own_at, step), columns]
            send[rows + to : rows + to + step, :] = terms[pl.ds(send_at, step), columns].astype(BF16)


def in_order(table, first, *pieces):
    n = len(pieces)
    for d, piece in enumerate(pieces):
        table[lax.rem(first + d, n)] = piece.astype(F32)
    total = table[0]
    for d in range(1, n):
        total = total + table[d]
    return total


def pair_kernel(own, recv, w_keep, *outs):
    rows, part = own.shape[0], w_keep.shape[0] // 4
    for d, out in enumerate(outs):
        n = (-d) % 4 * part
        out[:rows, :] = own[...]
        out[rows : 2 * rows, :] = recv[:rows]
        out[2 * rows :, :] = added(w_keep[n : n + part], recv[rows + n : rows + n + part])


def line_kernel(a, b, c, d, head, foot, whole):
    rows = whole.shape[0] // 4
    for k, ref in enumerate((a, b, c, d)):
        whole[k * rows : (k + 1) * rows, :] = ref[:rows]
        part = head if k < 2 else foot
        part[k % 2 * rows : (k % 2 + 1) * rows, :] = ref[:rows]
    head[2 * rows :, :] = added(*(ref[rows:] for ref in (a, b, c, d)))


def ring_kernel(up, up_term, down, down_term, up_out, down_out):
    rows = up_term.shape[0]
    for got, term, out in ((up, up_term, up_out), (down, down_term, down_out)):
        out[:rows, :] = added(got[:rows], term[...])
        out[rows:, :] = got[rows:]


def third_ring_kernel(up, up_term, down, own_term, up_out, own_out):
    rows = up_term.shape[0]
    up_out[:rows, :] = added(up[:rows], up_term[...])
    up_out[rows:, :] = up[rows:]
    own_out[...] = down[:rows].astype(F32) + own_term[...].astype(F32)


def last_ring_kernel(at_ref, up, own, w, up_1, up_2, up_3, down_1, down_2, down_3, w_out, out, table):
    rows = own.shape[0]
    tails = (ref[rows:] for ref in (down_1, down_2, down_3, up, up_3, up_2, up_1))
    w_out[...] = in_order(table, at_ref[0], w[...], *tails)
    total = added(up[:rows], own[...])
    width = total.shape[1]
    for c in range(out.shape[1] // width):
        out[:, c * width : (c + 1) * width] = total[c * out.shape[0] : (c + 1) * out.shape[0]]


def gather_kernel(at_ref, wa, wb, wc, wd, out):
    part = wa.shape[0]
    for d, piece in enumerate((wa, wb, wc, wd)):
        out[pl.ds(pl.multiple_of(lax.rem(at_ref[3] + d, 4) * part, part), part), :] = piece[...]


def weight_kernel(at_ref, mine, theirs, out):
    core, half = at_ref[1], out.shape[0] // 2
    step = half // 4
    for which, piece in ((core, mine), (1 - core, theirs)):
        for n in range(4):
            at = pl.ds(pl.multiple_of(which * half + n * step, step), step)
            for k in range(2):
                out[at, k * half : (k + 1) * half] = piece[(n * 2 + k) * step : (n * 2 + k + 1) * step]


def backward_kernel(nz, coord_ref, count_ref, at_ref, blocks_in, *refs):
    head, foot, minus_head, minus_foot, plus_head, plus_foot, low, high = refs[:8]
    line, first, second, last = refs[8:12]
    w, *outs = refs[12 : 13 + nz]
    blocks, back, acc, turned, table, sems = refs[13 + nz :]
    quarter = foot.shape[0]
    after = quarter + w.shape[0]
    mine = ((head, foot), (plus_head, plus_foot), (low, high), (minus_head, minus_foot))
    theirs = (
        (line.at[:quarter], line.at[quarter:]),
        (second.at[quarter : 2 * quarter], first.at[after:]),
        (last.at[:quarter], last.at[after:]),
        (first.at[:quarter], second.at[:quarter]),
    )
    size = blocks.shape[1]
    turns = blocks.shape[0] // UNROLL
    half = back.shape[2] // 2
    z, core = at_ref[0], at_ref[1]
    for t in range(turns):
        block_copy(blocks_in, blocks, sems, t).start()
    for sources, is_mine in ((mine, True), (theirs, False)):
        to = lanes(core if is_mine else 1 - core, half)
        for major in range(4):
            for minor in range(4):

                def read(q, carry, major=major, minor=minor, sources=sources, is_mine=is_mine, to=to):
                    at = pl.multiple_of((minor % 2 * 4 + q) * size, size)
                    if is_mine:
                        r = place(major, minor, 0, 0) + q
                    else:
                        r = place(minor, major, 0, 0) + jnp.bitwise_xor(q, 2)
                    back[r, :, to] = sources[major][minor // 2][pl.ds(at, size), :]
                    return carry

                lax.fori_loop(0, 4, read, 0)
    cols = acc.shape[0] - 1
    for c in range(cols):
        acc[c] = jnp.zeros(acc.shape[1:], F32)
    count = count_ref[0]

    def turn(t, carry):
        block_copy(blocks_in, blocks, sems, t).wait()
        for u in range(UNROLL):
            s = t * UNROLL + u
            c = jnp.where(s < count, coord_ref[1, s], cols)
            acc[c] += lax.dot_general(
                blocks[s], back[row_place(coord_ref, at_ref, s)], (((0,), (0,)), ((), ())), preferred_element_type=F32
            )
        return carry

    lax.fori_loop(0, turns, turn, 0)
    rows = w.shape[0]
    tails = (ref[quarter:] for ref in (head, plus_head, low, minus_head))
    w[...] = in_order(table, at_ref[2], *tails).astype(BF16)
    for out in (outs[4], outs[5]):
        out[out.shape[0] - rows :, :] = w[...]
    shard = turned.shape[1] // nz
    for c in range(cols):
        turned[c] = acc[c].astype(BF16).T
        for dz in range(nz):
            at = pl.multiple_of(lax.rem(z + dz, nz) * shard, shard)
            outs[dz][c * shard : (c + 1) * shard, :] = turned[c, pl.ds(at, shard), :]


def local(features, weight, cotangent, block_values, block_coords, block_counts):
    blocks, coords = block_values[0, 0], block_coords[0, 0]
    nz, ny = lax.axis_size("row"), lax.axis_size("rep")
    ncol = lax.axis_size("col")
    nx = ncol // CORES
    z, y = lax.axis_index("row"), lax.axis_index("rep")
    x, core = lax.axis_index("col") // CORES, lax.axis_index("col") % CORES
    at = jnp.stack([z, core, jnp.where(core == 0, x, y), jnp.where(core == 0, y, x)]).astype(jnp.int32)
    count = block_counts[0]
    coords = coords.T
    slots, size, _ = blocks.shape
    rows_dev, width = cotangent.shape
    half = width // 2
    nodes, shard = features.shape
    flops = 2 * slots * size * size * width
    turns = slots // UNROLL

    def move(a, axis, d):
        pairs = []
        for i in range(nx):
            for c in range(CORES):
                for j in range(ny):
                    along_x = (axis == "major") == (c == 0)
                    to = ((i + d) % nx, j) if along_x else (i, (j + d) % ny)
                    pairs.append(((i * CORES + c) * ny + j, (to[0] * CORES + c) * ny + to[1]))
        return lax.ppermute(a, ("col", "rep"), pairs)

    def swap(a):
        return lax.ppermute(a, "col", [(i, i ^ 1) for i in range(ncol)])

    def along_z(a, d):
        return lax.ppermute(a, "row", [(i, (i + d) % nz) for i in range(nz)])

    shards = [None] * nz
    shards[0] = features.T
    for k in range(1, nz // 2 + 1):
        shards[nz - k] = along_z(shards[(nz - k + 1) % nz], 1)
        if k < nz // 2:
            shards[k] = along_z(shards[k - 1], -1)

    (shards[0],) = call(
        own_kernel, (shards[0],), [shape((shard, nodes))], [pltpu.SemaphoreType.DMA], hbm=1
    )
    pair = CORES * rows_dev
    part_a = part_b = shape((8, pair, half))
    row_blocks = len(PLACES)
    send_a, send_b, keep_a, keep_b = call(
        functools.partial(forward_kernel, nz),
        (coords, count, at, blocks, *shards),
        [part_a, part_b, part_a, part_b],
        [
            pltpu.VMEM(blocks.shape, BF16),
            pltpu.VMEM((width, nodes), BF16),
            pltpu.VMEM((nodes // size, size, width), BF16),
            pltpu.VMEM((row_blocks + 1, size, width), F32),
            pltpu.SemaphoreType.DMA((turns,)),
        ],
        smem=3,
        hbm=1,
        limit=BIG,
        flops=flops,
    )

    recv_a = swap(send_a)
    two, one = shape((2, pair, half)), shape((pair, half))
    low, high, free_1, free_3, send_b = call(
        first_sum_kernel, (keep_a, recv_a, send_b), [two] * 4 + [part_b], aliases={2: 4}
    )
    low, high, recv_b = move(low, "major", 1), move(high, "major", -1), swap(send_b)
    free_1, free_3 = move(free_1, "major", 1), move(free_3, "major", -1)
    near_1, near_3 = call(second_sum_kernel, (keep_b, recv_b, low, high), [two] * 2)
    arrived = (free_1, free_3, move(near_1, "major", 1), move(near_3, "major", -1))
    sums = call(third_sum_kernel, (keep_b, recv_b, *arrived), [one] * 4)
    sums = [sums[0]] + [move(sums[d], "minor", d) for d in (1, 2, 3)]
    mine = shape((rows_dev, half))
    agg_own, agg_send = call(fourth_sum_kernel, sums, [mine] * 2)

    part = width // 4
    activations, back_own, send, w_keep = call(
        middle_kernel,
        (at, agg_own, swap(agg_send), weight, cotangent),
        [shape((rows_dev, width)), mine, shape((rows_dev + width, half)), shape((width, half), F32)],
        [pltpu.VMEM((rows_dev, width), BF16)] * 2 + [pltpu.VMEM((width, width), F32)],
        smem=1,
    )

    near = call(pair_kernel, (back_own, swap(send), w_keep), [shape((pair + part, half))] * 4)
    near = [near[0]] + [move(near[d], "minor", -d) for d in (1, 2, 3)]
    head, foot, line = call(
        line_kernel, near, [shape((2 * pair + part, half)), shape((2 * pair, half)), shape((4 * pair, half))]
    )
    minus_head, plus_foot = move(head, "major", 1), move(foot, "major", -1)
    minus_foot, plus_head = move(foot, "major", 1), move(head, "major", -1)
    low, high = move(minus_head, "major", 1), move(plus_foot, "major", -1)
    far = (minus_head, minus_foot, plus_head, plus_foot, low, high)
    merged = [jnp.concatenate(a) for a in ((minus_head, plus_foot), (minus_foot, plus_head), (low, high))]
    rows_all = (head, foot, *far, *(swap(a) for a in (line, *merged)))

    cells = shard * nodes // size
    ring, ring_w = shape((cells, size)), shape((cells + part, size))
    w, *terms = call(
        functools.partial(backward_kernel, nz),
        (coords, count, at, blocks, *rows_all),
        [shape((part, half))] + [ring_w if k in (4, 5) else ring for k in range(nz)],
        [
            pltpu.VMEM(blocks.shape, BF16),
            pltpu.VMEM((row_blocks, size, width), BF16),
            pltpu.VMEM((nodes // size + 1, size, width), F32),
            pltpu.VMEM((nodes // size, width, size), BF16),
            pltpu.VMEM((4, part, half), F32),
            pltpu.SemaphoreType.DMA((turns,)),
        ],
        smem=3,
        hbm=1,
        limit=BIG,
        flops=flops,
    )
    up_1, down_1 = along_z(terms[4], 1), along_z(terms[5], -1)
    up, down = call(ring_kernel, (up_1, terms[3], down_1, terms[6]), [ring_w] * 2)
    up_2, down_2 = along_z(up, 1), along_z(down, -1)
    up, down = call(ring_kernel, (up_2, terms[2], down_2, terms[7]), [ring_w] * 2)
    up_3, down_3 = along_z(up, 1), along_z(down, -1)
    up, own = call(
        third_ring_kernel,
        (up_3, terms[1], down_3, terms[0]),
        [ring_w, shape((cells, size), F32)],
    )
    w, input_grad = call(
        last_ring_kernel,
        (at, along_z(up, 1), own, w, up_1, up_2, up_3, down_1, down_2, down_3),
        [shape((part, half), F32), shape((shard, nodes))],
        [pltpu.VMEM((nz, part, half), F32)],
        smem=1,
    )
    w = [w] + [move(w, "minor", -d) for d in (1, 2, 3)]
    (w,) = call(gather_kernel, (at, *w), [shape((width, half), F32)], smem=1)
    (weight_grad,) = call(weight_kernel, (at, w, swap(w)), [shape((width, width), F32)], smem=1)
    return activations, input_grad.T, weight_grad


def solution(mesh):
    in_specs = (
        P(("col", "rep"), "row"),
        P(),
        P(("row", "col", "rep"), None),
        P("row", ("col", "rep"), None, None, None),
        P("row", ("col", "rep"), None, None),
        P("row", ("col", "rep")),
    )
    out_specs = (P(("row", "col", "rep"), None), P(("col", "rep"), "row"), P())
    return jax.shard_map(local, mesh=mesh, in_specs=in_specs, out_specs=out_specs, check_vma=False)
```
